32 devices in a mesh: pairs: 2 (over x), section: 2 (over core), tp: 8 (over z, y).
Axes of the slice: x: 2, y: 2, z: 4, core: 2. Of those that a mesh axis runs over, the one named last changes fastest.
Arguments:
- queries: bfloat16 [4, 96, 16384], P(('pairs', 'section'), None, 'tp'), parts along dimension 0, may hold values from -8 to 8, as said below
- fresh_key_value: bfloat16 [4, 96, 2, 8, 128], P(('pairs', 'section'), 'tp'), parts along dimension 0, may hold values from -6 to 6, as said below
- key_value_page_store: bfloat16 [4, 16, 2, 8, 128, 128], P(('pairs', 'section'), 'tp'), parts along dimension 0, may hold values from -6 to 6
- prefix_len: int32 [2], P('pairs'), parts along dimension 0, may hold values from 512 to 1024
- page_table: int32 [32, 4], P('pairs'), parts along dimension 0, may hold values from 0 to 23, as said below
- context_len: int32 [32], P('pairs'), parts along dimension 0, may hold values from 1 to 512, as said below
Outputs:
- attended: bfloat16 [4, 96, 16384], P(('pairs', 'section'), None, 'tp'), parts along dimension 0
The draws below stay inside these ranges and needn't reach their ends.
There are 2 independent parts, one for each index of `pairs`. The reference program is written for one: setup_inputs(seed, part) draws one part's arguments, and reference() takes and returns one part's arrays. A program takes and returns all parts, laid end to end along the dimension named above; each array names one. Nothing has to cross between parts.
Inputs may be any that keep to these rules, and one draw needn't show every extreme that they name: `queries`: mostly of order one; in a few rows of each side a query may match a key of its own side closely. `fresh_key_value`: mostly of order one. `page_table`: entries m of row r with m * 128 < context_len[r] are used; used entries are distinct over all rows; the others name any page and are not read. `context_len`: A row's length needs at most 4 pages.
All inputs are finite; a program needn't handle non-finite values.
Results may differ from the reference program's by a relative error of at most 0.0031.
Values may be sent and summed in bfloat16 or wider, within the bound.
No kernel may reach another device: no remote copies, remote signals or barrier semaphores. Data moves between devices by JAX's collectives and lax.ppermute only.
A program may use at most 128 MiB of HBM per device.

```python
import math
import jax
import jax.numpy as jnp
from jax import lax

QUERY_HEADS = 128
KEY_VALUE_HEADS = 8
HEAD_SIZE = 128
PAGE_POSITIONS = 128
PRE_DEV = 1
FIN_DEV = 1
MAXP = 4
DEVICE_PAGES = 2
DROWS = 16
QUERY_ROWS = 96
KEY_PAGE_SLOTS = 24
N_SECTION = 2
N_TP = 8


def ragged_table(key):
    first, second, third, fourth = jax.random.split(key, 4)
    extra = KEY_PAGE_SLOTS - MAXP - DROWS + 1
    ranks = jnp.arange(DROWS, dtype=jnp.int32)
    by_rank = jnp.where(ranks == 0, MAXP, jnp.where(ranks <= extra, 2, 1)).astype(jnp.int32)
    order = jax.random.permutation(first, DROWS)
    counts = jnp.zeros((DROWS,), jnp.int32).at[order].set(by_rank)
    starts = jnp.cumsum(counts) - counts
    slot_order = jax.random.permutation(second, KEY_PAGE_SLOTS).astype(jnp.int32)
    entries = jnp.arange(MAXP, dtype=jnp.int32)
    in_use = entries[None, :] < counts[:, None]
    picked = slot_order[jnp.clip(starts[:, None] + entries[None, :], 0, KEY_PAGE_SLOTS - 1)]
    filler = jax.random.randint(third, (DROWS, MAXP), 0, KEY_PAGE_SLOTS, dtype=jnp.int32)
    table = jnp.where(in_use, picked, filler)
    tails = jax.random.randint(fourth, (DROWS,), 1, PAGE_POSITIONS + 1, dtype=jnp.int32)
    lengths = jnp.where(counts == MAXP, MAXP * PAGE_POSITIONS, (counts - 1) * PAGE_POSITIONS + tails)
    return (table, lengths.astype(jnp.int32))


def draw_queries(key, part):
    key = jax.random.fold_in(key, 3)
    array_extent = (N_SECTION, QUERY_ROWS, QUERY_HEADS * HEAD_SIZE)
    values = jnp.clip(2.0 * jax.random.normal(key, array_extent, jnp.float32), -8.0, 8.0)
    return values.astype(jnp.bfloat16)


def draw_fresh_key_value(key, part):
    key = jax.random.fold_in(key, 4)
    array_extent = (N_SECTION, QUERY_ROWS, 2, KEY_VALUE_HEADS, HEAD_SIZE)
    values = jnp.clip(jax.random.normal(key, array_extent, jnp.float32), -6.0, 6.0)
    return values.astype(jnp.bfloat16)


def draw_page_table(key, part):
    shared = ragged_table(key)
    return shared[0]


def draw_context_len(key, part):
    shared = ragged_table(key)
    return shared[1]


def steps_of(key, shape, pieces, low, largest):
    gain = 1.0
    for axis_at, parts in pieces:
        heights = jax.random.uniform(jax.random.fold_in(jax.random.fold_in(key, 6), axis_at), (parts,), jnp.float32, low / len(pieces), largest / len(pieces))
        gain = gain * jnp.repeat(jnp.exp(heights), shape[axis_at] // parts).reshape((-1,) + (1,) * (len(shape) - 1 - axis_at))
    return gain


def bell_draw(stream_key, extent, width, reach, shards=(), kind=jnp.bfloat16):
    gain = steps_of(stream_key, extent, shards, -0.22, 0.18) if shards else 1.0
    values = jax.random.normal(stream_key, extent, jnp.float32) * width * gain
    return jnp.minimum(jnp.maximum(values, -reach), reach).astype(kind)


def setup_inputs(seed: int = 0, part: int = 0) -> dict:
    streams_of = jax.random.split(jax.random.key(seed), 7)
    part_splits = jax.random.split(jax.random.fold_in(streams_of[6], part), 7)
    return {
        "queries": draw_queries(jax.random.fold_in(jax.random.fold_in(streams_of[6], part), 71), part),
        "fresh_key_value": draw_fresh_key_value(jax.random.fold_in(jax.random.fold_in(streams_of[6], part), 71), part),
        "key_value_page_store": bell_draw(part_splits[2], (N_SECTION, N_TP * DEVICE_PAGES, 2, KEY_VALUE_HEADS, PAGE_POSITIONS, HEAD_SIZE), 1.0, 6.0, ((0, 2), (1, 8))),
        "prefix_len": jax.random.randint(part_splits[3], (1,), N_TP * PRE_DEV * PAGE_POSITIONS // 2, N_TP * PRE_DEV * PAGE_POSITIONS + 1).astype(jnp.int32),
        "page_table": draw_page_table(jax.random.fold_in(jax.random.fold_in(streams_of[6], part), 71), part),
        "context_len": draw_context_len(jax.random.fold_in(jax.random.fold_in(streams_of[6], part), 71), part),
    }


def build_visible(is_prefill, prefix_len, page_table, context_len, slot_count, per_device, prefix_pages, page_size, row_count):
    dec_rows, max_entries = page_table.shape
    key_index = jnp.arange(slot_count * page_size, dtype=jnp.int32)
    slot_of = key_index // page_size
    within = key_index % page_size
    device_of = slot_of // per_device
    local_of = slot_of % per_device
    prefix_pos = (device_of * prefix_pages + local_of) * page_size + within
    prefix_end = prefix_len[0]
    prefix_ok = (local_of < prefix_pages) & (prefix_pos < prefix_end)
    entries = jnp.arange(max_entries, dtype=jnp.int32)
    in_use = entries[None, :] * page_size < context_len[:, None]
    matches = (page_table[:, :, None] == jnp.arange(slot_count, dtype=jnp.int32)[None, None, :]) & in_use[:, :, None]
    match_int = matches.astype(jnp.int32)
    row_ids = jnp.arange(dec_rows, dtype=jnp.int32)
    owned = lax.optimization_barrier(jnp.sum(match_int, axis=(0, 1))) > 0
    owners = lax.optimization_barrier(jnp.sum(match_int * row_ids[:, None, None], axis=(0, 1)))
    offsets = lax.optimization_barrier(jnp.sum(match_int * (entries * page_size)[None, :, None], axis=(0, 1)))
    limits = lax.optimization_barrier(jnp.sum(match_int * context_len[:, None, None], axis=(0, 1)))
    decode_pos = jnp.repeat(offsets, page_size) + within
    decode_ok = jnp.repeat(owned, page_size) & (decode_pos < jnp.repeat(limits, page_size))
    decode_seq = jnp.repeat(owners, page_size)
    step_count = row_count // dec_rows
    query_index = jnp.arange(row_count, dtype=jnp.int32)
    decode_row = jnp.tile(row_ids, step_count)
    decode_qpos = jnp.tile(context_len, step_count) + query_index // dec_rows
    key_ok = jnp.where(is_prefill, prefix_ok, decode_ok)
    key_seq = jnp.where(is_prefill, 0, decode_seq)
    query_seq = jnp.where(is_prefill, 0, decode_row)
    query_pos = jnp.where(is_prefill, prefix_end + query_index, decode_qpos)
    cached = key_ok[None, :] & (key_seq[None, :] == query_seq[:, None])
    fresh = (query_seq[None, :] == query_seq[:, None]) & (query_pos[None, :] <= query_pos[:, None])
    return jnp.concatenate([cached, fresh], axis=1)

def attend_head(head_query, key_rows, value_rows, visible, factor):
    scores = lax.dot_general(head_query, key_rows, (((1,), (1,)), ((), ())), preferred_element_type=jnp.float32) * factor
    scores = jnp.where(visible, scores, -1e+30)
    highest = lax.optimization_barrier(jnp.max(scores, axis=1, keepdims=True))
    raw_weights = jnp.exp(scores - highest)
    denominator = lax.optimization_barrier(jnp.sum(raw_weights, axis=1, keepdims=True))
    weights = raw_weights.astype(jnp.bfloat16)
    return (jnp.dot(weights, value_rows, preferred_element_type=jnp.float32) / denominator).astype(jnp.bfloat16)

def reference(queries, fresh_key_value, key_value_page_store, prefix_len, page_table, context_len):
    page_stores = key_value_page_store.reshape((2, N_TP, DEVICE_PAGES, 2, KEY_VALUE_HEADS, PAGE_POSITIONS, HEAD_SIZE))
    finished = page_stores[0, :, PRE_DEV:]
    factor = 1.0 / math.sqrt(HEAD_SIZE)
    query_group_width = QUERY_HEADS // KEY_VALUE_HEADS
    results = []
    for group_number in range(2):
        pages_landed = jnp.zeros_like(finished) if group_number == 0 else finished
        merged_output = jnp.concatenate([page_stores[group_number], pages_landed], axis=1).reshape((KEY_PAGE_SLOTS, 2, KEY_VALUE_HEADS, PAGE_POSITIONS, HEAD_SIZE))
        key_gathered = jnp.concatenate([merged_output[:, 0].transpose(1, 0, 2, 3).reshape((KEY_VALUE_HEADS, KEY_PAGE_SLOTS * PAGE_POSITIONS, HEAD_SIZE)), fresh_key_value[group_number, :, 0].transpose(1, 0, 2)], axis=1)
        value_gathered = jnp.concatenate([merged_output[:, 1].transpose(1, 0, 2, 3).reshape((KEY_VALUE_HEADS, KEY_PAGE_SLOTS * PAGE_POSITIONS, HEAD_SIZE)), fresh_key_value[group_number, :, 1].transpose(1, 0, 2)], axis=1)
        visible = build_visible(group_number == 0, prefix_len, page_table, context_len, KEY_PAGE_SLOTS, DEVICE_PAGES + FIN_DEV, PRE_DEV, PAGE_POSITIONS, QUERY_ROWS)
        side_queries = queries[group_number]

        def one_head(head_index):
            kv_index = head_index // query_group_width
            head_query = lax.dynamic_slice_in_dim(side_queries, head_index * HEAD_SIZE, HEAD_SIZE, axis=1)
            return attend_head(head_query, key_gathered[kv_index], value_gathered[kv_index], visible, factor)
        per_head = lax.map(one_head, jnp.arange(QUERY_HEADS, dtype=jnp.int32))
        results.append(per_head.transpose(1, 0, 2).reshape((QUERY_ROWS, QUERY_HEADS * HEAD_SIZE)))
    return jnp.stack(results)
```

```python
import functools
import math

import jax
import jax.numpy as jnp
from jax import lax
from jax.experimental import pallas as pl
from jax.experimental.pallas import tpu as pltpu
from jax.sharding import PartitionSpec as P

FIN_DEV = 1
ROW_TILE = 16
MASKED = -1e30
LOG2_E = 1.4426950408889634


def round_up(value, multiple):
    return -(-value // multiple) * multiple


def shift_pairs(size, by):
    return [(i, (i + by) % size) for i in range(size)]


def dot_keys(left, keys):
    return lax.dot_general(
        left, keys, (((1,), (1,)), ((), ())), preferred_element_type=jnp.float32
    )


def weigh(scores, scale):
    highest = jnp.max(scores, axis=1, keepdims=True)
    raw = jnp.exp2((scores - highest) * scale)
    return raw, jnp.sum(raw, axis=1, keepdims=True)


def attend_kernel(
    sizes,
    meta_ref,
    prefix_ref,
    table_ref,
    context_ref,
    queries_ref,
    row_queries_ref,
    *refs,
):
    tp, pages_here, page, new_rows, new_pad, dec_rows, steps, heads = sizes
    prefix_pages = pages_here - FIN_DEV
    per_device = pages_here + FIN_DEV
    chunks, relayed = refs[:tp], refs[tp : 2 * tp]
    out_ref, keys_ref, values_ref, new_keys_ref, new_values_ref, held_ref, sems = refs[2 * tp :]
    me = meta_ref[1]
    head_dim = queries_ref.shape[1] // heads
    scale = LOG2_E / math.sqrt(head_dim)
    row_count = steps * dec_rows
    new_at = pages_here * 2 * page

    def source(d):
        return lax.rem(me + tp - d, tp)

    def load(pages_of):
        copies = []
        for d in range(tp):
            for chunk, at, slot in pages_of(d, source(d)):
                copies.append((chunk.at[pl.ds(at, page)], keys_ref.at[slot]))
                copies.append((chunk.at[pl.ds(at + page, page)], values_ref.at[slot]))
            rows = pl.ds(pl.multiple_of(source(d) * new_pad, new_pad), new_pad)
            copies.append((chunks[d].at[pl.ds(new_at, new_pad)], new_keys_ref.at[rows]))
            copies.append(
                (chunks[d].at[pl.ds(new_at + new_pad, new_pad)], new_values_ref.at[rows])
            )
        started = [
            pltpu.make_async_copy(src, dst, sems.at[i]) for i, (src, dst) in enumerate(copies)
        ]
        for copy in started:
            copy.start()
        for copy in started:
            copy.wait()

    column = lax.broadcasted_iota(jnp.int32, (1, tp * new_pad), 1)
    new_index = (column // new_pad) * new_rows + lax.rem(column, new_pad)
    new_real = lax.rem(column, new_pad) < new_rows

    @pl.when(meta_ref[0] == 0)
    def prefill():
        load(
            lambda d, j: [
                (chunks[d], q * 2 * page, j * prefix_pages + q) for q in range(prefix_pages)
            ]
        )
        cached = tp * prefix_pages
        key_rows = keys_ref[:cached].reshape((cached * page, head_dim))
        value_rows = values_ref[:cached].reshape((cached * page, head_dim))
        cached_ok = (
            lax.broadcasted_iota(jnp.int32, (1, cached * page), 1) < prefix_ref[0]
        )
        query_index = lax.broadcasted_iota(jnp.int32, (row_count, 1), 0)
        new_ok = new_real & (new_index <= query_index)

        def one_head(h, carry):
            columns = pl.ds(pl.multiple_of(h * head_dim, head_dim), head_dim)
            query = queries_ref[:, columns]
            scores = jnp.where(cached_ok, dot_keys(query, key_rows), MASKED)
            new_scores = jnp.where(new_ok, dot_keys(query, new_keys_ref[...]), MASKED)
            highest = jnp.maximum(
                jnp.max(scores, axis=1, keepdims=True), jnp.max(new_scores, axis=1, keepdims=True)
            )
            raw = jnp.exp2((scores - highest) * scale)
            new_raw = jnp.exp2((new_scores - highest) * scale)
            total = jnp.sum(raw, axis=1, keepdims=True) + jnp.sum(new_raw, axis=1, keepdims=True)
            summed = jnp.dot(
                raw.astype(jnp.bfloat16), value_rows, preferred_element_type=jnp.float32
            ) + jnp.dot(
                new_raw.astype(jnp.bfloat16),
                new_values_ref[...],
                preferred_element_type=jnp.float32,
            )
            out_ref[:, columns] = (summed / total).astype(out_ref.dtype)
            return carry

        lax.fori_loop(0, heads, one_head, 0)

    @pl.when(meta_ref[0] != 0)
    def decode():
        load(
            lambda d, j: [
                (chunks[d], q * 2 * page, j * per_device + q) for q in range(pages_here)
            ]
            + [
                (relayed[d], (prefix_pages + q) * 2 * page, j * per_device + pages_here + q)
                for q in range(FIN_DEV)
            ]
        )
        row_pad = row_queries_ref.shape[1]
        max_entries = table_ref.shape[1]
        slot = lax.broadcasted_iota(jnp.int32, (1, page), 1)
        query_step = lax.broadcasted_iota(jnp.int32, (row_pad, 1), 0) // heads
        new_row = jnp.where(new_real, lax.rem(new_index, dec_rows), -1)
        new_early = (new_index // dec_rows) <= query_step

        def one_row(r, carry):
            query = row_queries_ref[r]
            length = context_ref[r]
            slots = [
                jnp.clip(table_ref[r, m], 0, tp * per_device - 1) for m in range(max_entries)
            ]
            scores = [
                jnp.where(slot < length - m * page, dot_keys(query, keys_ref[slots[m]]), MASKED)
                for m in range(max_entries)
            ]
            scores.append(
                jnp.where(
                    new_early & (new_row == r), dot_keys(query, new_keys_ref[...]), MASKED
                )
            )
            raw, total = weigh(jnp.concatenate(scores, axis=1), scale)
            raw = raw.astype(jnp.bfloat16)
            summed = jnp.dot(
                raw[:, max_entries * page :],
                new_values_ref[...],
                preferred_element_type=jnp.float32,
            )
            for m in range(max_entries):
                summed += jnp.dot(
                    raw[:, m * page : (m + 1) * page],
                    values_ref[slots[m]],
                    preferred_element_type=jnp.float32,
                )
            held_ref[pl.ds(pl.multiple_of(r * row_pad, row_pad), row_pad), :] = summed / total
            return carry

        lax.fori_loop(0, dec_rows, one_row, 0)
        for s in range(steps):
            for h in range(heads):
                out_ref[s * dec_rows : (s + 1) * dec_rows, h * head_dim : (h + 1) * head_dim] = (
                    held_ref[pl.ds(s * heads + h, dec_rows, stride=row_pad), :]
                ).astype(out_ref.dtype)


def attend(meta, prefix_len, page_table, context_len, queries, chunks, relayed, sizes):
    tp, pages_here, page, new_rows, new_pad, dec_rows, steps, heads = sizes
    row_count, width = queries.shape
    head_dim = width // heads
    row_pad = round_up(steps * heads, ROW_TILE)
    row_queries = queries.reshape((steps, dec_rows, heads, head_dim)).transpose(1, 0, 2, 3)
    row_queries = row_queries.reshape((dec_rows, steps * heads, head_dim))
    row_queries = jnp.pad(row_queries, ((0, 0), (0, row_pad - steps * heads), (0, 0)))
    slots = tp * (pages_here + FIN_DEV)
    smem = pl.BlockSpec(memory_space=pltpu.SMEM)
    vmem = pl.BlockSpec(memory_space=pltpu.VMEM)
    anywhere = pl.BlockSpec(memory_space=pl.ANY)
    flops = 4 * row_count * width * (tp * page + row_count)
    return pl.pallas_call(
        functools.partial(attend_kernel, sizes),
        out_shape=jax.ShapeDtypeStruct((row_count, width), queries.dtype),
        in_specs=[smem] * 4 + [vmem] * 2 + [anywhere] * (2 * tp),
        out_specs=vmem,
        scratch_shapes=[
            pltpu.VMEM((slots, page, head_dim), queries.dtype),
            pltpu.VMEM((slots, page, head_dim), queries.dtype),
            pltpu.VMEM((tp * new_pad, head_dim), queries.dtype),
            pltpu.VMEM((tp * new_pad, head_dim), queries.dtype),
            pltpu.VMEM((dec_rows * row_pad, head_dim), jnp.float32),
            pltpu.SemaphoreType.DMA((tp * (2 * (pages_here + FIN_DEV) + 2),)),
        ],
        compiler_params=pltpu.CompilerParams(vmem_limit_bytes=40 * 1024 * 1024),
        cost_estimate=pl.CostEstimate(
            flops=flops, bytes_accessed=4 * slots * page * head_dim, transcendentals=0
        ),
        name="attend",
    )(meta, prefix_len, page_table, context_len, queries, row_queries, *chunks, *relayed)


def body(queries, fresh_key_value, key_value_page_store, prefix_len, page_table, context_len):
    tp = lax.axis_size("tp")
    section, me = lax.axis_index("section"), lax.axis_index("tp")
    store, fresh = key_value_page_store[0], fresh_key_value[0]
    pages_here, _, kv_heads, page, head_dim = store.shape
    new_rows = fresh.shape[0]
    new_pad = round_up(new_rows, ROW_TILE)
    heads = queries.shape[2] // head_dim
    dec_rows = page_table.shape[0]
    steps = queries.shape[1] // dec_rows

    def chunk_for(device):
        head = device * kv_heads // tp
        pages = lax.dynamic_index_in_dim(store, head, axis=2, keepdims=False)
        new = lax.dynamic_index_in_dim(fresh, head, axis=2, keepdims=False).transpose(1, 0, 2)
        new = jnp.pad(new, ((0, 0), (0, new_pad - new_rows), (0, 0)))
        return jnp.concatenate([pages.reshape((-1, head_dim)), new.reshape((-1, head_dim))])

    chunks = [chunk_for(me)]
    for d in range(1, tp):
        chunks.append(
            lax.ppermute(chunk_for(lax.rem(me + d, tp)), "tp", shift_pairs(tp, d))
        )
    relayed = [lax.ppermute(chunk, "section", [(0, 1), (1, 0)]) for chunk in chunks]
    sizes = (tp, pages_here, page, new_rows, new_pad, dec_rows, steps, heads)
    meta = jnp.stack([section, me]).astype(jnp.int32)
    out = attend(meta, prefix_len, page_table, context_len, queries[0], chunks, relayed, sizes)
    return out[None]


def solution(mesh):
    placed = (
        P(("pairs", "section"), None, "tp"),
        P(("pairs", "section"), "tp", None, None, None),
        P(("pairs", "section"), "tp", None, None, None, None),
        P("pairs"),
        P("pairs", None),
        P("pairs"),
    )
    return jax.shard_map(
        body,
        mesh=mesh,
        in_specs=placed,
        out_specs=P(("pairs", "section"), None, "tp"),
        check_vma=False,
    )
```

```python
import functools
import math

import jax
import jax.numpy as jnp
from jax import lax
from jax.experimental import pallas as pl
from jax.experimental.pallas import tpu as pltpu
from jax.sharding import PartitionSpec as P

FIN_DEV = 1
ROW_TILE = 16
LANES = 128
BLOCK_BATCH = 4
MASKED = -1e30
LOG2_E = 1.4426950408889634


def round_up(value, multiple):
    return -(-value // multiple) * multiple


def shift_pairs(size, by):
    return [(i, (i + by) % size) for i in range(size)]


class Sizes:
    def __init__(self, tp, store, fresh, queries, page_table):
        self.tp = tp
        self.pages_here, _, self.kv_heads, self.page, self.head_dim = store
        self.prefix_pages = self.pages_here - FIN_DEV
        self.per_device = self.pages_here + FIN_DEV
        self.new_rows = fresh[0]
        self.new_pad = round_up(self.new_rows, ROW_TILE)
        self.new_keys = tp * self.new_pad
        self.heads = queries[1] // self.head_dim
        self.row_count = queries[0]
        self.dec_rows, self.max_entries = page_table
        self.steps = self.row_count // self.dec_rows
        self.slots = tp * self.per_device
        self.scale = LOG2_E / math.sqrt(self.head_dim)
        self.new_at = self.pages_here * 2 * self.page
        self.prefill_tiles = round_up(self.heads * self.row_count, LANES) // LANES
        self.row_width = round_up(self.steps * self.heads, LANES)
        self.row_tiles = self.row_width // LANES
        self.decode_tiles = self.dec_rows * self.row_tiles
        self.tiles = max(self.prefill_tiles, self.decode_tiles)
        self.prefix_at = 2
        self.context_at = 3
        self.table_at = 3 + self.dec_rows

    def source(self, meta_ref, d):
        return lax.rem(meta_ref[1] + self.tp - d, self.tp)


def score(keys, queries):
    return lax.dot_general(
        keys, queries, (((1,), (1,)), ((), ())), preferred_element_type=jnp.float32
    )


def soften(scores, values, scale):
    highest = jnp.max(scores, axis=0, keepdims=True)
    raw = jnp.exp2((scores - highest) * scale)
    total = jnp.sum(raw, axis=0, keepdims=True)
    summed = lax.dot_general(
        values,
        raw.astype(values.dtype),
        (((0,), (0,)), ((), ())),
        preferred_element_type=jnp.float32,
    )
    return summed, highest, total


def merge(first, second, scale):
    highest = jnp.maximum(first[1], second[1])
    keep = jnp.exp2((first[1] - highest) * scale)
    add = jnp.exp2((second[1] - highest) * scale)
    return (
        first[0] * keep + second[0] * add,
        highest,
        first[2] * keep + second[2] * add,
    )


def read(state, tile):
    return tuple(ref[tile] for ref in state)


def write(state, tile, part):
    for ref, value in zip(state, part):
        ref[tile] = value


def settle(part):
    return (part[0] * (1.0 / part[2])).T


def key_rows(z, count):
    return lax.broadcasted_iota(jnp.int32, (count, LANES), 0)


def add_pages(z, pages, owner_ref, valid_ref, queries_ref, state):
    slot = key_rows(z, z.page)
    for start in range(0, len(pages), BLOCK_BATCH):
        parts = []
        for ref, at, number in pages[start : start + BLOCK_BATCH]:
            visible = slot < valid_ref[number]
            keys, values = ref[at : at + z.page, :], ref[at + z.page : at + 2 * z.page, :]
            for i in range(z.row_tiles):
                tile = owner_ref[number] * z.row_tiles + i
                scores = jnp.where(visible, score(keys, queries_ref[tile]), MASKED)
                parts.append((tile, soften(scores, values, z.scale)))
        for tile, part in parts:
            write(state, tile, merge(read(state, tile), part, z.scale))


def prefix_visible(z, meta_ref, shifts):
    slot = key_rows(z, z.page)
    return [
        slot < meta_ref[z.prefix_at] - (z.source(meta_ref, d) * z.prefix_pages + q) * z.page
        for d in shifts
        for q in range(z.prefix_pages)
    ]


def prefix_rows(z, chunks, shifts, which):
    return [
        chunks[d][(2 * q + which) * z.page : (2 * q + which + 1) * z.page, :]
        for d in shifts
        for q in range(z.prefix_pages)
    ]


def new_rows(z, new_ref, chunks, which):
    sources = [(new_ref, at) for at in range(0, new_ref.shape[0], 2 * z.new_pad)]
    sources += [(chunk, z.new_at) for chunk in chunks]
    rows = [pl.ds(at + which * z.new_pad, z.new_pad) for _, at in sources]
    return [ref[span, :] for (ref, _), span in zip(sources, rows)]


def new_index(z, meta_ref, shifts):
    within = key_rows(z, z.new_pad)
    none = jnp.full_like(within, z.row_count)
    return jnp.concatenate(
        [
            jnp.where(within < z.new_rows, z.source(meta_ref, d) * z.new_rows + within, none)
            for d in shifts
        ],
        axis=0,
    )


def local_pages(z, meta_ref, chunks, shifts):
    return [
        (chunks[d], 2 * q * z.page, z.source(meta_ref, d) * z.per_device + q)
        for d in shifts
        for q in range(z.pages_here)
    ]


def landed_pages(z, meta_ref, landed_ref, shifts):
    return [
        (
            landed_ref,
            2 * (i * FIN_DEV + q) * z.page,
            z.source(meta_ref, d) * z.per_device + z.pages_here + q,
        )
        for i, d in enumerate(shifts)
        for q in range(FIN_DEV)
    ]


def first_kernel(z, shifts, meta_ref, prefill_ref, decode_ref, *refs):
    chunks = dict(zip(shifts, refs))
    owner_ref, valid_ref, packed_ref, new_ref = refs[len(shifts) : len(shifts) + 4]
    state = refs[len(shifts) + 4 :]
    first, last = z.prefix_pages * 2 * z.page, z.new_at
    for i, d in enumerate(shifts):
        packed_ref[i * (last - first) : (i + 1) * (last - first), :] = chunks[d][first:last, :]
        new_ref[i * 2 * z.new_pad : (i + 1) * 2 * z.new_pad, :] = chunks[d][z.new_at :, :]

    def forget(n, carry):
        owner_ref[n] = 0
        valid_ref[n] = 0
        return carry

    def note(r, carry):
        length = meta_ref[z.context_at + r]
        for m in range(z.max_entries):

            @pl.when(m * z.page < length)
            def used():
                number = meta_ref[z.table_at + r * z.max_entries + m]
                number = jnp.clip(number, 0, z.slots - 1)
                owner_ref[number] = r
                valid_ref[number] = jnp.minimum(length - m * z.page, z.page)

        return carry

    lax.fori_loop(0, z.slots, forget, 0)
    lax.fori_loop(0, z.dec_rows, note, 0)

    @pl.when(meta_ref[0] == 0)
    def prefill():
        visible = jnp.concatenate(prefix_visible(z, meta_ref, shifts), axis=0)
        keys = jnp.concatenate(prefix_rows(z, chunks, shifts, 0), axis=0)
        values = jnp.concatenate(prefix_rows(z, chunks, shifts, 1), axis=0)
        for tile in range(z.prefill_tiles):
            scores = jnp.where(visible, score(keys, prefill_ref[tile]), MASKED)
            write(state, tile, soften(scores, values, z.scale))

    @pl.when(meta_ref[0] != 0)
    def decode():
        state[0][...] = jnp.zeros_like(state[0])
        state[1][...] = jnp.full_like(state[1], MASKED)
        state[2][...] = jnp.zeros_like(state[2])
        pages = local_pages(z, meta_ref, chunks, shifts)
        add_pages(z, pages, owner_ref, valid_ref, decode_ref, state)


def second_kernel(z, groups, meta_ref, owner_ref, valid_ref, prefill_ref, decode_ref, *refs):
    shifts = groups[1]
    before, new_ref, refs = refs[:3], refs[3], refs[4:]
    late, state, out_ref, held_ref = refs[: len(shifts)], refs[len(shifts) : -2], refs[-2], refs[-1]
    chunks = dict(zip(shifts, late))
    index = new_index(z, meta_ref, groups[0] + groups[1])
    column = lax.broadcasted_iota(jnp.int32, (1, LANES), 1)
    new_keys = jnp.concatenate(new_rows(z, new_ref, late, 0), axis=0)

    @pl.when(meta_ref[0] == 0)
    def prefill():
        visible = jnp.concatenate(prefix_visible(z, meta_ref, shifts), axis=0)
        keys = jnp.concatenate(prefix_rows(z, chunks, shifts, 0), axis=0)
        values = prefix_rows(z, chunks, shifts, 1) + new_rows(z, new_ref, late, 1)
        values = jnp.concatenate(values, axis=0)
        for tile in range(z.prefill_tiles):
            query = lax.rem(column + tile * LANES, z.row_count)
            scores = jnp.concatenate(
                [
                    jnp.where(visible, score(keys, prefill_ref[tile]), MASKED),
                    jnp.where(index <= query, score(new_keys, prefill_ref[tile]), MASKED),
                ],
                axis=0,
            )
            part = merge(read(before, tile), soften(scores, values, z.scale), z.scale)
            held_ref[tile * LANES : (tile + 1) * LANES, :] = settle(part).astype(held_ref.dtype)
        for h in range(z.heads):
            out_ref[:, h * z.head_dim : (h + 1) * z.head_dim] = held_ref[
                h * z.row_count : (h + 1) * z.row_count, :
            ]

    @pl.when(meta_ref[0] != 0)
    def decode():
        owner = lax.rem(index, z.dec_rows)
        owner = jnp.where(index < z.row_count, owner, -1)
        step = index // z.dec_rows
        new_values = jnp.concatenate(new_rows(z, new_ref, late, 1), axis=0)
        for tile in range(z.decode_tiles):
            row, i = divmod(tile, z.row_tiles)
            query = (column + i * LANES) // z.heads
            visible = (owner == row) & (step <= query)
            scores = jnp.where(visible, score(new_keys, decode_ref[tile]), MASKED)
            part = soften(scores, new_values, z.scale)
            write(state, tile, merge(read(before, tile), part, z.scale))
        pages = local_pages(z, meta_ref, chunks, shifts)
        add_pages(z, pages, owner_ref, valid_ref, decode_ref, state)


def last_kernel(z, groups, meta_ref, owner_ref, valid_ref, decode_ref, *refs):
    landed, refs = refs[: len(groups)], refs[len(groups) :]
    before, done_ref, out_ref, state, held_ref = refs[:3], refs[3], refs[4], refs[5:8], refs[8]

    @pl.when(meta_ref[0] == 0)
    def prefill():
        out_ref[...] = done_ref[...]

    @pl.when(meta_ref[0] != 0)
    def decode():
        for ref, value in zip(state, before):
            ref[...] = value[...]
        pages = []
        for ref, shifts in zip(landed, groups):
            pages += landed_pages(z, meta_ref, ref, shifts)
        add_pages(z, pages, owner_ref, valid_ref, decode_ref, state)
        for tile in range(z.decode_tiles):
            held_ref[tile * LANES : (tile + 1) * LANES, :] = settle(read(state, tile))
        for s in range(z.steps):
            for h in range(z.heads):
                rows = pl.ds(s * z.heads + h, z.dec_rows, stride=z.row_width)
                out_ref[
                    s * z.dec_rows : (s + 1) * z.dec_rows,
                    h * z.head_dim : (h + 1) * z.head_dim,
                ] = held_ref[rows, :].astype(out_ref.dtype)


def call(kernel, z, shifts, name, keys, operands, outputs, scratch=()):
    spaces = {"smem": pltpu.SMEM, "vmem": pltpu.VMEM}
    spec = {key: pl.BlockSpec(memory_space=space) for key, space in spaces.items()}
    return pl.pallas_call(
        functools.partial(kernel, z, shifts),
        out_shape=[shape for _, shape in outputs],
        in_specs=[spec[key] for key, _ in operands],
        out_specs=[spec[key] for key, _ in outputs],
        scratch_shapes=list(scratch),
        compiler_params=pltpu.CompilerParams(vmem_limit_bytes=24 * 1024 * 1024),
        cost_estimate=pl.CostEstimate(
            flops=4 * z.tiles * LANES * keys * z.head_dim,
            bytes_accessed=2 * z.tiles * LANES * z.head_dim * 8,
            transcendentals=z.tiles * LANES * keys,
        ),
        name=name,
    )(*[value for _, value in operands])


def query_tiles(z, queries):
    by_head = queries.reshape((z.row_count, z.heads, z.head_dim)).transpose(1, 0, 2)
    by_head = by_head.reshape((-1, z.head_dim))
    spare = z.prefill_tiles * LANES - by_head.shape[0]
    by_head = jnp.pad(by_head, ((0, spare), (0, 0)))
    by_row = queries.reshape((z.steps, z.dec_rows, z.heads, z.head_dim)).transpose(1, 0, 2, 3)
    by_row = by_row.reshape((z.dec_rows, z.steps * z.heads, z.head_dim))
    by_row = jnp.pad(by_row, ((0, 0), (0, z.row_width - z.steps * z.heads), (0, 0)))
    return (
        by_head.reshape((z.prefill_tiles, LANES, z.head_dim)),
        by_row.reshape((z.decode_tiles, LANES, z.head_dim)),
    )


def hand_over(pages):
    return lax.ppermute(pages, "section", [(0, 1), (1, 0)])


def finished(z, chunks):
    first, last = z.prefix_pages * 2 * z.page, z.new_at
    return jnp.concatenate([chunk[first:last] for chunk in chunks], axis=0)


def attend(z, meta, queries, chunks, early, late):
    prefill, decode = query_tiles(z, queries)
    table = ("smem", jax.ShapeDtypeStruct((z.slots,), jnp.int32))
    state = [
        ("vmem", jax.ShapeDtypeStruct((z.tiles, rows, LANES), jnp.float32))
        for rows in (z.head_dim, 1, 1)
    ]
    out = ("vmem", jax.ShapeDtypeStruct(queries.shape, queries.dtype))
    owner, valid, packed, new, *first = call(
        first_kernel,
        z,
        early,
        "early_pages",
        len(early) * z.page,
        [("smem", meta), ("vmem", prefill), ("vmem", decode)]
        + [("vmem", chunks[d]) for d in early],
        [table, table]
        + [
            ("vmem", jax.ShapeDtypeStruct((len(early) * rows, z.head_dim), queries.dtype))
            for rows in (FIN_DEV * 2 * z.page, 2 * z.new_pad)
        ]
        + state,
    )
    *waiting, owner = lax.optimization_barrier((*chunks, owner))
    landed = [hand_over(packed), hand_over(finished(z, [waiting[d] for d in late]))]
    common = [("smem", meta), ("smem", owner), ("smem", valid)]
    *second, done = call(
        second_kernel,
        z,
        (early, late),
        "late_pages",
        len(late) * z.page + z.new_keys,
        common
        + [("vmem", value) for value in (prefill, decode, *first, new)]
        + [("vmem", waiting[d]) for d in late],
        state + [out],
        [pltpu.VMEM((z.prefill_tiles * LANES, z.head_dim), queries.dtype)],
    )
    (result,) = call(
        last_kernel,
        z,
        (early, late),
        "landed_pages",
        z.page,
        common + [("vmem", value) for value in (decode, *landed, *second, done)],
        [out],
        [pltpu.VMEM(shape.shape, shape.dtype) for _, shape in state]
        + [pltpu.VMEM((z.decode_tiles * LANES, z.head_dim), jnp.float32)],
    )
    return result


def body(queries, fresh_key_value, key_value_page_store, prefix_len, page_table, context_len):
    tp = lax.axis_size("tp")
    section, me = lax.axis_index("section"), lax.axis_index("tp")
    store, fresh = key_value_page_store[0], fresh_key_value[0]
    z = Sizes(tp, store.shape, fresh.shape, queries.shape[1:], page_table.shape)

    def chunk_for(device):
        head = device * z.kv_heads // tp
        pages = lax.dynamic_index_in_dim(store, head, axis=2, keepdims=False)
        new = lax.dynamic_index_in_dim(fresh, head, axis=2, keepdims=False).transpose(1, 0, 2)
        new = jnp.pad(new, ((0, 0), (0, z.new_pad - z.new_rows), (0, 0)))
        return jnp.concatenate([pages.reshape((-1, z.head_dim)), new.reshape((-1, z.head_dim))])

    chunks = [chunk_for(me)]
    for d in range(1, tp):
        chunks.append(lax.ppermute(chunk_for(lax.rem(me + d, tp)), "tp", shift_pairs(tp, d)))
    early = [0, tp - 2] + list(range(1, tp // 2 - 1))
    late = [d for d in range(tp) if d not in early]
    meta = jnp.concatenate(
        [
            jnp.stack([section, me]).astype(jnp.int32),
            prefix_len,
            context_len,
            page_table.reshape((-1,)),
        ]
    )
    return attend(z, meta, queries[0], chunks, early, late)[None]


def solution(mesh):
    placed = (
        P(("pairs", "section"), None, "tp"),
        P(("pairs", "section"), "tp", None, None, None),
        P(("pairs", "section"), "tp", None, None, None, None),
        P("pairs"),
        P("pairs", None),
        P("pairs"),
    )
    return jax.shard_map(
        body,
        mesh=mesh,
        in_specs=placed,
        out_specs=P(("pairs", "section"), None, "tp"),
        check_vma=False,
    )
```

```python
import functools
import math

import jax
import jax.numpy as jnp
from jax import lax
from jax.experimental import pallas as pl
from jax.experimental.pallas import tpu as pltpu
from jax.sharding import PartitionSpec as P

FIN_DEV = 1
ROW_TILE = 16
LANES = 128
BLOCK_BATCH = 4
MASKED = -1e30
LOG2_E = 1.4426950408889634


def round_up(value, multiple):
    return -(-value // multiple) * multiple


def shift_pairs(size, by):
    return [(i, (i + by) % size) for i in range(size)]


class Sizes:
    def __init__(self, tp, store, fresh, queries, page_table):
        self.tp = tp
        self.pages_here, _, self.kv_heads, self.page, self.head_dim = store
        self.prefix_pages = self.pages_here - FIN_DEV
        self.per_device = self.pages_here + FIN_DEV
        self.new_rows = fresh[0]
        self.new_pad = round_up(self.new_rows, ROW_TILE)
        self.new_keys = tp * self.new_pad
        self.heads = queries[1] // self.head_dim
        self.row_count = queries[0]
        self.dec_rows, self.max_entries = page_table
        self.steps = self.row_count // self.dec_rows
        self.slots = tp * self.per_device
        self.scale = LOG2_E / math.sqrt(self.head_dim)
        self.new_at = self.pages_here * 2 * self.page
        self.prefill_tiles = round_up(self.heads * self.row_count, LANES) // LANES
        self.row_width = round_up(self.steps * self.heads, LANES)
        self.row_tiles = self.row_width // LANES
        self.decode_tiles = self.dec_rows * self.row_tiles
        self.tiles = max(self.prefill_tiles, self.decode_tiles)
        self.prefix_at = 2
        self.context_at = 3
        self.table_at = 3 + self.dec_rows

    def source(self, meta_ref, d):
        return lax.rem(meta_ref[1] + self.tp - d, self.tp)


def score(keys, queries):
    return jnp.dot(keys, queries, preferred_element_type=jnp.float32)


def soften(scores, values, scale):
    highest = jnp.max(scores, axis=0, keepdims=True)
    raw = jnp.exp2((scores - highest) * scale)
    total = jnp.sum(raw, axis=0, keepdims=True)
    summed = lax.dot_general(
        values,
        raw.astype(values.dtype),
        (((0,), (0,)), ((), ())),
        preferred_element_type=jnp.float32,
    )
    return summed, highest, total


def merge(first, second, scale):
    highest = jnp.maximum(first[1], second[1])
    keep = jnp.exp2((first[1] - highest) * scale)
    add = jnp.exp2((second[1] - highest) * scale)
    return (
        first[0] * keep + second[0] * add,
        highest,
        first[2] * keep + second[2] * add,
    )


def read(state, tile):
    return tuple(ref[tile] for ref in state)


def write(state, tile, part):
    for ref, value in zip(state, part):
        ref[tile] = value


def settle(part):
    return (part[0] * (1.0 / part[2])).T


def key_rows(z, count):
    return lax.broadcasted_iota(jnp.int32, (count, LANES), 0)


def add_pages(z, pages, owner_ref, valid_ref, queries_ref, state):
    slot = key_rows(z, z.page)
    for start in range(0, len(pages), BLOCK_BATCH):
        parts = []
        for ref, at, number in pages[start : start + BLOCK_BATCH]:
            visible = slot < valid_ref[number]
            keys, values = ref[at : at + z.page, :], ref[at + z.page : at + 2 * z.page, :]
            for i in range(z.row_tiles):
                tile = owner_ref[number] * z.row_tiles + i
                scores = jnp.where(visible, score(keys, queries_ref[tile]), MASKED)
                parts.append((tile, soften(scores, values, z.scale)))
        for tile, part in parts:
            write(state, tile, merge(read(state, tile), part, z.scale))


def prefix_visible(z, meta_ref, shifts):
    slot = key_rows(z, z.page)
    return [
        slot < meta_ref[z.prefix_at] - (z.source(meta_ref, d) * z.prefix_pages + q) * z.page
        for d in shifts
        for q in range(z.prefix_pages)
    ]


def prefix_rows(z, chunks, shifts, which):
    return [
        chunks[d][(2 * q + which) * z.page : (2 * q + which + 1) * z.page, :]
        for d in shifts
        for q in range(z.prefix_pages)
    ]


def new_rows(z, new_ref, chunks, which):
    sources = [(new_ref, at) for at in range(0, new_ref.shape[0], 2 * z.new_pad)]
    sources += [(chunk, z.new_at) for chunk in chunks]
    rows = [pl.ds(at + which * z.new_pad, z.new_pad) for _, at in sources]
    return [ref[span, :] for (ref, _), span in zip(sources, rows)]


def new_index(z, meta_ref, shifts):
    within = key_rows(z, z.new_pad)
    none = jnp.full_like(within, z.row_count)
    return jnp.concatenate(
        [
            jnp.where(within < z.new_rows, z.source(meta_ref, d) * z.new_rows + within, none)
            for d in shifts
        ],
        axis=0,
    )


def local_pages(z, meta_ref, chunks, shifts):
    return [
        (chunks[d], 2 * q * z.page, z.source(meta_ref, d) * z.per_device + q)
        for d in shifts
        for q in range(z.pages_here)
    ]


def landed_pages(z, meta_ref, landed_ref, shifts):
    return [
        (
            landed_ref,
            2 * (i * FIN_DEV + q) * z.page,
            z.source(meta_ref, d) * z.per_device + z.pages_here + q,
        )
        for i, d in enumerate(shifts)
        for q in range(FIN_DEV)
    ]


def pack(z, chunks, packed_ref):
    first, last = z.prefix_pages * 2 * z.page, z.new_at
    for i, chunk in enumerate(chunks):
        packed_ref[i * (last - first) : (i + 1) * (last - first), :] = chunk[first:last, :]


def pack_kernel(z, shifts, owner_ref, *refs):
    pack(z, refs[:-1], refs[-1])


def first_kernel(z, shifts, meta_ref, prefill_ref, decode_ref, *refs):
    chunks = dict(zip(shifts, refs))
    owner_ref, valid_ref, packed_ref, new_ref = refs[len(shifts) : len(shifts) + 4]
    state = refs[len(shifts) + 4 :]
    pack(z, refs[: len(shifts)], packed_ref)
    for i, d in enumerate(shifts):
        new_ref[i * 2 * z.new_pad : (i + 1) * 2 * z.new_pad, :] = chunks[d][z.new_at :, :]

    def forget(n, carry):
        owner_ref[n] = 0
        valid_ref[n] = 0
        return carry

    def note(r, carry):
        length = meta_ref[z.context_at + r]
        for m in range(z.max_entries):

            @pl.when(m * z.page < length)
            def used():
                number = meta_ref[z.table_at + r * z.max_entries + m]
                number = jnp.clip(number, 0, z.slots - 1)
                owner_ref[number] = r
                valid_ref[number] = jnp.minimum(length - m * z.page, z.page)

        return carry

    lax.fori_loop(0, z.slots, forget, 0)
    lax.fori_loop(0, z.dec_rows, note, 0)

    @pl.when(meta_ref[0] == 0)
    def prefill():
        visible = jnp.concatenate(prefix_visible(z, meta_ref, shifts), axis=0)
        keys = jnp.concatenate(prefix_rows(z, chunks, shifts, 0), axis=0)
        values = jnp.concatenate(prefix_rows(z, chunks, shifts, 1), axis=0)
        for tile in range(z.prefill_tiles):
            scores = jnp.where(visible, score(keys, prefill_ref[tile]), MASKED)
            write(state, tile, soften(scores, values, z.scale))

    @pl.when(meta_ref[0] != 0)
    def decode():
        state[0][...] = jnp.zeros_like(state[0])
        state[1][...] = jnp.full_like(state[1], MASKED)
        state[2][...] = jnp.zeros_like(state[2])
        pages = local_pages(z, meta_ref, chunks, shifts)
        add_pages(z, pages, owner_ref, valid_ref, decode_ref, state)


def second_kernel(z, groups, meta_ref, owner_ref, valid_ref, prefill_ref, decode_ref, *refs):
    shifts = groups[1]
    before, new_ref, refs = refs[:3], refs[3], refs[4:]
    late, state, out_ref, held_ref = refs[: len(shifts)], refs[len(shifts) : -2], refs[-2], refs[-1]
    chunks = dict(zip(shifts, late))
    index = new_index(z, meta_ref, groups[0] + groups[1])
    column = lax.broadcasted_iota(jnp.int32, (1, LANES), 1)
    new_keys = jnp.concatenate(new_rows(z, new_ref, late, 0), axis=0)

    @pl.when(meta_ref[0] == 0)
    def prefill():
        visible = jnp.concatenate(prefix_visible(z, meta_ref, shifts), axis=0)
        keys = prefix_rows(z, chunks, shifts, 0)
        cached = len(keys) * z.page
        keys = jnp.concatenate(keys + new_rows(z, new_ref, late, 0), axis=0)
        values = prefix_rows(z, chunks, shifts, 1) + new_rows(z, new_ref, late, 1)
        values = jnp.concatenate(values, axis=0)
        for tile in range(z.prefill_tiles):
            query = lax.rem(column + tile * LANES, z.row_count)
            scores = score(keys, prefill_ref[tile])
            scores = jnp.concatenate(
                [
                    jnp.where(visible, scores[:cached], MASKED),
                    jnp.where(index <= query, scores[cached:], MASKED),
                ],
                axis=0,
            )
            part = merge(read(before, tile), soften(scores, values, z.scale), z.scale)
            held_ref[tile * LANES : (tile + 1) * LANES, :] = settle(part).astype(held_ref.dtype)
        for h in range(z.heads):
            out_ref[:, h * z.head_dim : (h + 1) * z.head_dim] = held_ref[
                h * z.row_count : (h + 1) * z.row_count, :
            ]

    @pl.when(meta_ref[0] != 0)
    def decode():
        owner = lax.rem(index, z.dec_rows)
        owner = jnp.where(index < z.row_count, owner, -1)
        step = index // z.dec_rows
        new_values = jnp.concatenate(new_rows(z, new_ref, late, 1), axis=0)
        for tile in range(z.decode_tiles):
            row, i = divmod(tile, z.row_tiles)
            query = (column + i * LANES) // z.heads
            visible = (owner == row) & (step <= query)
            scores = jnp.where(visible, score(new_keys, decode_ref[tile]), MASKED)
            part = soften(scores, new_values, z.scale)
            write(state, tile, merge(read(before, tile), part, z.scale))
        pages = local_pages(z, meta_ref, chunks, shifts)
        add_pages(z, pages, owner_ref, valid_ref, decode_ref, state)


def last_kernel(z, groups, meta_ref, owner_ref, valid_ref, decode_ref, *refs):
    landed, refs = refs[: len(groups)], refs[len(groups) :]
    before, done_ref, out_ref, state, held_ref = refs[:3], refs[3], refs[4], refs[5:8], refs[8]

    @pl.when(meta_ref[0] == 0)
    def prefill():
        out_ref[...] = done_ref[...]

    @pl.when(meta_ref[0] != 0)
    def decode():
        for ref, value in zip(state, before):
            ref[...] = value[...]
        pages = []
        for ref, shifts in zip(landed, groups):
            pages += landed_pages(z, meta_ref, ref, shifts)
        add_pages(z, pages, owner_ref, valid_ref, decode_ref, state)
        for tile in range(z.decode_tiles):
            held_ref[tile * LANES : (tile + 1) * LANES, :] = settle(read(state, tile))
        for s in range(z.steps):
            for h in range(z.heads):
                rows = pl.ds(s * z.heads + h, z.dec_rows, stride=z.row_width)
                out_ref[
                    s * z.dec_rows : (s + 1) * z.dec_rows,
                    h * z.head_dim : (h + 1) * z.head_dim,
                ] = held_ref[rows, :].astype(out_ref.dtype)


def call(kernel, z, shifts, name, keys, operands, outputs, scratch=()):
    spaces = {"smem": pltpu.SMEM, "vmem": pltpu.VMEM}
    spec = {key: pl.BlockSpec(memory_space=space) for key, space in spaces.items()}
    return pl.pallas_call(
        functools.partial(kernel, z, shifts),
        out_shape=[shape for _, shape in outputs],
        in_specs=[spec[key] for key, _ in operands],
        out_specs=[spec[key] for key, _ in outputs],
        scratch_shapes=list(scratch),
        compiler_params=pltpu.CompilerParams(vmem_limit_bytes=16 * 1024 * 1024),
        cost_estimate=pl.CostEstimate(
            flops=4 * z.tiles * LANES * keys * z.head_dim,
            bytes_accessed=2 * z.tiles * LANES * z.head_dim * 8,
            transcendentals=z.tiles * LANES * keys,
        ),
        name=name,
    )(*[value for _, value in operands])


def query_tiles(z, queries):
    by_head = queries.reshape((z.row_count, z.heads, z.head_dim)).transpose(1, 0, 2)
    by_head = by_head.reshape((-1, z.head_dim))
    spare = z.prefill_tiles * LANES - by_head.shape[0]
    by_head = jnp.pad(by_head, ((0, spare), (0, 0)))
    by_row = queries.reshape((z.steps, z.dec_rows, z.heads, z.head_dim)).transpose(1, 0, 2, 3)
    by_row = by_row.reshape((z.dec_rows, z.steps * z.heads, z.head_dim))
    by_row = jnp.pad(by_row, ((0, 0), (0, z.row_width - z.steps * z.heads), (0, 0)))
    return (
        by_head.reshape((z.prefill_tiles, LANES, z.head_dim)).transpose(0, 2, 1),
        by_row.reshape((z.decode_tiles, LANES, z.head_dim)).transpose(0, 2, 1),
    )


def hand_over(pages):
    return lax.ppermute(pages, "section", [(0, 1), (1, 0)])


def attend(z, meta, queries, chunks, early, late):
    prefill, decode = query_tiles(z, queries)
    table = ("smem", jax.ShapeDtypeStruct((z.slots,), jnp.int32))
    state = [
        ("vmem", jax.ShapeDtypeStruct((z.tiles, rows, LANES), jnp.float32))
        for rows in (z.head_dim, 1, 1)
    ]
    def packed_shape(count):
        rows = count * FIN_DEV * 2 * z.page
        return ("vmem", jax.ShapeDtypeStruct((rows, z.head_dim), queries.dtype))

    out = ("vmem", jax.ShapeDtypeStruct(queries.shape, queries.dtype))
    owner, valid, packed, new, *first = call(
        first_kernel,
        z,
        early,
        "early_pages",
        len(early) * z.page,
        [("smem", meta), ("vmem", prefill), ("vmem", decode)]
        + [("vmem", chunks[d]) for d in early],
        [table, table, packed_shape(len(early))]
        + [("vmem", jax.ShapeDtypeStruct((len(early) * 2 * z.new_pad, z.head_dim), queries.dtype))]
        + state,
    )
    *waiting, owner = lax.optimization_barrier((*chunks, owner))
    (late_packed,) = call(
        pack_kernel,
        z,
        late,
        "pack_late",
        1,
        [("smem", owner)] + [("vmem", chunks[d]) for d in late],
        [packed_shape(len(late))],
    )
    landed = [hand_over(packed), hand_over(late_packed)]
    common = [("smem", meta), ("smem", owner), ("smem", valid)]
    *second, done = call(
        second_kernel,
        z,
        (early, late),
        "late_pages",
        len(late) * z.page + z.new_keys,
        common
        + [("vmem", value) for value in (prefill, decode, *first, new)]
        + [("vmem", chunks[d]) for d in late],
        state + [out],
        [pltpu.VMEM((z.prefill_tiles * LANES, z.head_dim), queries.dtype)],
    )
    (result,) = call(
        last_kernel,
        z,
        (early, late),
        "landed_pages",
        z.page,
        common + [("vmem", value) for value in (decode, *landed, *second, done)],
        [out],
        [pltpu.VMEM(shape.shape, shape.dtype) for _, shape in state]
        + [pltpu.VMEM((z.decode_tiles * LANES, z.head_dim), jnp.float32)],
    )
    return result


def body(queries, fresh_key_value, key_value_page_store, prefix_len, page_table, context_len):
    tp = lax.axis_size("tp")
    section, me = lax.axis_index("section"), lax.axis_index("tp")
    store, fresh = key_value_page_store[0], fresh_key_value[0]
    z = Sizes(tp, store.shape, fresh.shape, queries.shape[1:], page_table.shape)

    def chunk_for(device):
        head = device * z.kv_heads // tp
        pages = lax.dynamic_index_in_dim(store, head, axis=2, keepdims=False)
        new = lax.dynamic_index_in_dim(fresh, head, axis=2, keepdims=False).transpose(1, 0, 2)
        new = jnp.pad(new, ((0, 0), (0, z.new_pad - z.new_rows), (0, 0)))
        return jnp.concatenate([pages.reshape((-1, z.head_dim)), new.reshape((-1, z.head_dim))])

    chunks = [chunk_for(me)]
    for d in range(1, tp):
        chunks.append(lax.ppermute(chunk_for(lax.rem(me + d, tp)), "tp", shift_pairs(tp, d)))
    early = [0, tp - 2] + list(range(1, tp // 2 - 1))
    late = [d for d in range(tp) if d not in early]
    meta = jnp.concatenate(
        [
            jnp.stack([section, me]).astype(jnp.int32),
            prefix_len,
            context_len,
            page_table.reshape((-1,)),
        ]
    )
    return attend(z, meta, queries[0], chunks, early, late)[None]


def solution(mesh):
    placed = (
        P(("pairs", "section"), None, "tp"),
        P(("pairs", "section"), "tp", None, None, None),
        P(("pairs", "section"), "tp", None, None, None, None),
        P("pairs"),
        P("pairs", None),
        P("pairs"),
    )
    return jax.shard_map(
        body,
        mesh=mesh,
        in_specs=placed,
        out_specs=P(("pairs", "section"), None, "tp"),
        check_vma=False,
    )
```

```python
import functools
import math

import jax
import jax.numpy as jnp
from jax import lax
from jax.experimental import pallas as pl
from jax.experimental.pallas import tpu as pltpu
from jax.sharding import PartitionSpec as P

FIN_DEV = 1
ROW_TILE = 16
LANES = 128
BLOCK_BATCH = 4
MASKED = -1e30
LOG2_E = 1.4426950408889634


def round_up(value, multiple):
    return -(-value // multiple) * multiple


class Sizes:
    def __init__(self, tp, store, fresh, queries, page_table):
        self.tp = tp
        self.pages_here, _, self.kv_heads, self.page, self.head_dim = store
        self.prefix_pages = self.pages_here - FIN_DEV
        self.per_device = self.pages_here + FIN_DEV
        self.new_rows = fresh[0]
        self.new_pad = round_up(self.new_rows, ROW_TILE)
        self.new_keys = tp * self.new_pad
        self.heads = queries[1] // self.head_dim
        self.row_count = queries[0]
        self.dec_rows, self.max_entries = page_table
        self.steps = self.row_count // self.dec_rows
        self.slots = tp * self.per_device
        self.scale = LOG2_E / math.sqrt(self.head_dim)
        self.new_at = self.pages_here * 2 * self.page
        self.prefill_tiles = round_up(self.heads * self.row_count, LANES) // LANES
        self.row_width = round_up(self.steps * self.heads, LANES)
        self.row_tiles = self.row_width // LANES
        self.decode_tiles = self.dec_rows * self.row_tiles
        self.tiles = max(self.prefill_tiles, self.decode_tiles)
        self.owner_at = 1
        self.valid_at = 1 + self.slots

    def source(self, d):
        return lax.rem(lax.axis_index("tp") + self.tp - d, self.tp)

    def target(self, d):
        return lax.rem(lax.axis_index("tp") + d, self.tp)

    def pairs(self, d):
        return [(i, (i + d) % self.tp) for i in range(self.tp)]


def score(keys, queries):
    return jnp.dot(keys, queries, preferred_element_type=jnp.float32)


def soften(scores, values, scale):
    highest = jnp.max(scores, axis=0, keepdims=True)
    raw = jnp.exp2((scores - highest) * scale)
    total = jnp.sum(raw, axis=0, keepdims=True)
    summed = lax.dot_general(
        values,
        raw.astype(values.dtype),
        (((0,), (0,)), ((), ())),
        preferred_element_type=jnp.float32,
    )
    return summed, highest, total


def merge(first, second, scale):
    highest = jnp.maximum(first[1], second[1])
    keep = jnp.exp2((first[1] - highest) * scale)
    add = jnp.exp2((second[1] - highest) * scale)
    return (
        first[0] * keep + second[0] * add,
        highest,
        first[2] * keep + second[2] * add,
    )


def read(state, tile):
    return tuple(ref[tile] for ref in state)


def write(state, tile, part):
    for ref, value in zip(state, part):
        ref[tile] = value


def settle(part):
    return (part[0] * (1.0 / part[2])).T


def key_rows(z, count):
    return lax.broadcasted_iota(jnp.int32, (count, LANES), 0)


def add_pages(z, pages, plan_ref, queries_ref, state):
    slot = key_rows(z, z.page)
    for start in range(0, len(pages), BLOCK_BATCH):
        parts = []
        for ref, at, number in pages[start : start + BLOCK_BATCH]:
            visible = slot < plan_ref[z.valid_at + number]
            keys, values = ref[at : at + z.page, :], ref[at + z.page : at + 2 * z.page, :]
            for i in range(z.row_tiles):
                tile = plan_ref[z.owner_at + number] * z.row_tiles + i
                scores = jnp.where(visible, score(keys, queries_ref[tile]), MASKED)
                parts.append((tile, soften(scores, values, z.scale)))
        for tile, part in parts:
            write(state, tile, merge(read(state, tile), part, z.scale))


def prefix_visible(z, plan_ref, shifts):
    slot = key_rows(z, z.page)
    return [
        slot < plan_ref[0] - (z.source(d) * z.prefix_pages + q) * z.page
        for d in shifts
        for q in range(z.prefix_pages)
    ]


def prefix_rows(z, chunks, shifts, which):
    return [
        chunks[d][(2 * q + which) * z.page : (2 * q + which + 1) * z.page, :]
        for d in shifts
        for q in range(z.prefix_pages)
    ]


def new_rows(z, new_ref, chunks, which):
    sources = [(new_ref, at) for at in range(0, new_ref.shape[0], 2 * z.new_pad)]
    sources += [(chunk, z.new_at) for chunk in chunks]
    rows = [pl.ds(at + which * z.new_pad, z.new_pad) for _, at in sources]
    return [ref[span, :] for (ref, _), span in zip(sources, rows)]


def new_index(z, shifts):
    within = key_rows(z, z.new_pad)
    none = jnp.full_like(within, z.row_count)
    return jnp.concatenate(
        [
            jnp.where(within < z.new_rows, z.source(d) * z.new_rows + within, none)
            for d in shifts
        ],
        axis=0,
    )


def local_pages(z, chunks, shifts):
    return [
        (chunks[d], 2 * q * z.page, z.source(d) * z.per_device + q)
        for d in shifts
        for q in range(z.pages_here)
    ]


def landed_pages(z, places, shifts):
    return [
        (ref, at + 2 * q * z.page, z.source(d) * z.per_device + z.pages_here + q)
        for (ref, at), d in zip(places, shifts)
        for q in range(FIN_DEV)
    ]


def on_side(side):
    return pl.when(lax.axis_index("section") == side)


def first_kernel(
    z, shifts, prefix_ref, table_ref, context_ref, prefill_ref, decode_ref, *refs
):
    chunks, refs = dict(zip(shifts, refs)), refs[len(shifts) :]
    plan_ref, packed_ref, new_ref, state = refs[0], refs[1], refs[2], refs[3:]
    first, last = z.prefix_pages * 2 * z.page, z.new_at
    for i, d in enumerate(shifts):
        packed_ref[i * (last - first) : (i + 1) * (last - first), :] = chunks[d][first:last, :]
        new_ref[i * 2 * z.new_pad : (i + 1) * 2 * z.new_pad, :] = chunks[d][z.new_at :, :]

    def forget(n, carry):
        plan_ref[z.owner_at + n] = 0
        plan_ref[z.valid_at + n] = 0
        return carry

    def note(r, carry):
        length = context_ref[r]
        for m in range(z.max_entries):

            @pl.when(m * z.page < length)
            def used():
                number = jnp.clip(table_ref[m, r], 0, z.slots - 1)
                plan_ref[z.owner_at + number] = r
                plan_ref[z.valid_at + number] = jnp.minimum(length - m * z.page, z.page)

        return carry

    plan_ref[0] = prefix_ref[0]
    lax.fori_loop(0, z.slots, forget, 0)
    lax.fori_loop(0, z.dec_rows, note, 0)

    @on_side(0)
    def prefill():
        visible = jnp.concatenate(prefix_visible(z, plan_ref, shifts), axis=0)
        keys = jnp.concatenate(prefix_rows(z, chunks, shifts, 0), axis=0)
        values = jnp.concatenate(prefix_rows(z, chunks, shifts, 1), axis=0)
        for tile in range(z.prefill_tiles):
            scores = jnp.where(visible, score(keys, prefill_ref[tile]), MASKED)
            write(state, tile, soften(scores, values, z.scale))

    @on_side(1)
    def decode():
        state[0][...] = jnp.zeros_like(state[0])
        state[1][...] = jnp.full_like(state[1], MASKED)
        state[2][...] = jnp.zeros_like(state[2])
        pages = local_pages(z, chunks, shifts)
        add_pages(z, pages, plan_ref, decode_ref, state)


def second_kernel(z, groups, plan_ref, prefill_ref, decode_ref, *refs):
    shifts = groups[1]
    before, new_ref, refs = refs[:3], refs[3], refs[4:]
    late, refs = refs[: len(shifts)], refs[len(shifts) :]
    state, (out_ref, held_ref, sems) = refs[:3], refs[3:]
    chunks = dict(zip(shifts, late))
    index = new_index(z, groups[0] + groups[1])
    column = lax.broadcasted_iota(jnp.int32, (1, LANES), 1)
    new_keys = jnp.concatenate(new_rows(z, new_ref, late, 0), axis=0)

    @on_side(0)
    def prefill():
        visible = jnp.concatenate(prefix_visible(z, plan_ref, shifts), axis=0)
        keys = prefix_rows(z, chunks, shifts, 0)
        cached = len(keys) * z.page
        keys = jnp.concatenate(keys + new_rows(z, new_ref, late, 0), axis=0)
        values = prefix_rows(z, chunks, shifts, 1) + new_rows(z, new_ref, late, 1)
        values = jnp.concatenate(values, axis=0)
        copies = []
        for tile in range(z.prefill_tiles):
            query = lax.rem(column + tile * LANES, z.row_count)
            scores = score(keys, prefill_ref[tile])
            scores = jnp.concatenate(
                [
                    jnp.where(visible, scores[:cached], MASKED),
                    jnp.where(index <= query, scores[cached:], MASKED),
                ],
                axis=0,
            )
            part = merge(read(before, tile), soften(scores, values, z.scale), z.scale)
            held_ref[tile * LANES : (tile + 1) * LANES, :] = settle(part).astype(held_ref.dtype)
            while len(copies) < min((tile + 1) * LANES // z.row_count, z.heads):
                h = len(copies)
                source = held_ref.at[pl.ds(h * z.row_count, z.row_count)]
                target = out_ref.at[:, pl.ds(h * z.head_dim, z.head_dim)]
                copies.append(pltpu.make_async_copy(source, target, sems.at[h]))
                copies[-1].start()
        for copy in copies:
            copy.wait()

    @on_side(1)
    def decode():
        owner = lax.rem(index, z.dec_rows)
        owner = jnp.where(index < z.row_count, owner, -1)
        step = index // z.dec_rows
        new_values = jnp.concatenate(new_rows(z, new_ref, late, 1), axis=0)
        for tile in range(z.decode_tiles):
            row, i = divmod(tile, z.row_tiles)
            query = (column + i * LANES) // z.heads
            visible = (owner == row) & (step <= query)
            scores = jnp.where(visible, score(new_keys, decode_ref[tile]), MASKED)
            part = soften(scores, new_values, z.scale)
            write(state, tile, merge(read(before, tile), part, z.scale))
        pages = local_pages(z, chunks, shifts)
        add_pages(z, pages, plan_ref, decode_ref, state)


def last_kernel(z, groups, plan_ref, decode_ref, early_ref, *refs):
    late, refs = refs[: len(groups[1])], refs[len(groups[1]) :]
    before, out_ref, refs = refs[:3], refs[4], refs[5:]
    state, (held_ref, rows_ref, sems) = refs[:3], refs[3:]

    @on_side(1)
    def decode():
        for ref, value in zip(state, before):
            ref[...] = value[...]
        places = [(early_ref, i * FIN_DEV * 2 * z.page) for i in range(len(groups[0]))]
        places += [(ref, z.prefix_pages * 2 * z.page) for ref in late]
        pages = landed_pages(z, places, groups[0] + groups[1])
        add_pages(z, pages, plan_ref, decode_ref, state)
        for tile in range(z.decode_tiles):
            held_ref[tile * LANES : (tile + 1) * LANES, :] = settle(read(state, tile))
        copies = []
        for s in range(z.steps):
            span = pl.ds(s * z.dec_rows, z.dec_rows)
            for h in range(z.heads):
                rows = pl.ds(s * z.heads + h, z.dec_rows, stride=z.row_width)
                rows_ref[span, h * z.head_dim : (h + 1) * z.head_dim] = held_ref[rows, :].astype(
                    rows_ref.dtype
                )
            copies.append(
                pltpu.make_async_copy(rows_ref.at[span], out_ref.at[span], sems.at[s])
            )
            copies[-1].start()
        for copy in copies:
            copy.wait()


def call(kernel, z, shifts, name, keys, operands, outputs, scratch=(), aliases=None):
    spaces = {"smem": pltpu.SMEM, "vmem": pltpu.VMEM, "any": pl.ANY}
    spec = {key: pl.BlockSpec(memory_space=space) for key, space in spaces.items()}
    return pl.pallas_call(
        functools.partial(kernel, z, shifts),
        out_shape=[shape for _, shape in outputs],
        in_specs=[spec[key] for key, _ in operands],
        out_specs=[spec[key] for key, _ in outputs],
        scratch_shapes=list(scratch),
        input_output_aliases=aliases or {},
        compiler_params=pltpu.CompilerParams(vmem_limit_bytes=16 * 1024 * 1024),
        cost_estimate=pl.CostEstimate(
            flops=4 * z.tiles * LANES * keys * z.head_dim,
            bytes_accessed=2 * z.tiles * LANES * z.head_dim * 8,
            transcendentals=z.tiles * LANES * keys,
        ),
        name=name,
    )(*[value for _, value in operands])


def query_tiles(z, queries):
    by_head = queries.reshape((z.row_count, z.heads, z.head_dim)).transpose(1, 0, 2)
    by_head = by_head.reshape((-1, z.head_dim))
    spare = z.prefill_tiles * LANES - by_head.shape[0]
    by_head = jnp.pad(by_head, ((0, spare), (0, 0)))
    by_row = queries.reshape((z.steps, z.dec_rows, z.heads, z.head_dim)).transpose(1, 0, 2, 3)
    by_row = by_row.reshape((z.dec_rows, z.steps * z.heads, z.head_dim))
    by_row = jnp.pad(by_row, ((0, 0), (0, z.row_width - z.steps * z.heads), (0, 0)))
    return (
        by_head.reshape((z.prefill_tiles, LANES, z.head_dim)).transpose(0, 2, 1),
        by_row.reshape((z.decode_tiles, LANES, z.head_dim)).transpose(0, 2, 1),
    )


def hand_over(pages):
    return lax.ppermute(pages, "section", [(0, 1), (1, 0)])


def attend(z, inputs, queries, chunks, early, late):
    prefill, decode = query_tiles(z, queries)

    def shaped(space, shape, dtype):
        return (space, jax.ShapeDtypeStruct(shape, dtype))

    state = [
        shaped("vmem", (z.tiles, rows, LANES), jnp.float32) for rows in (z.head_dim, 1, 1)
    ]
    out = shaped("any", queries.shape, queries.dtype)
    plan, packed, new, *first = call(
        first_kernel,
        z,
        early,
        "early_pages",
        len(early) * z.page,
        [("smem", value) for value in inputs]
        + [("vmem", value) for value in (prefill, decode)]
        + [("vmem", chunks[d]) for d in early],
        [shaped("smem", (1 + 2 * z.slots,), jnp.int32)]
        + [
            shaped("vmem", (len(early) * rows, z.head_dim), queries.dtype)
            for rows in (FIN_DEV * 2 * z.page, 2 * z.new_pad)
        ]
        + state,
    )
    *waiting, plan = lax.optimization_barrier((*[chunks[d] for d in early + late], plan))
    landed = [hand_over(packed)] + [hand_over(chunk) for chunk in waiting[len(early) :]]
    *second, done = call(
        second_kernel,
        z,
        (early, late),
        "late_pages",
        len(late) * z.page + z.new_keys,
        [("smem", plan)]
        + [("vmem", value) for value in (prefill, decode, *first, new)]
        + [("vmem", chunks[d]) for d in late],
        state + [out],
        [
            pltpu.VMEM((z.prefill_tiles * LANES, z.head_dim), queries.dtype),
            pltpu.SemaphoreType.DMA((z.heads,)),
        ],
    )
    operands = [("smem", plan)]
    operands += [("vmem", value) for value in (decode, *landed, *second)]
    (result,) = call(
        last_kernel,
        z,
        (early, late),
        "landed_pages",
        z.page,
        operands + [("any", done)],
        [out],
        [pltpu.VMEM(shape.shape, shape.dtype) for _, shape in state]
        + [
            pltpu.VMEM((z.decode_tiles * LANES, z.head_dim), jnp.float32),
            pltpu.VMEM(queries.shape, queries.dtype),
            pltpu.SemaphoreType.DMA((z.steps,)),
        ],
        {len(operands): 0},
    )
    return result


def body(queries, fresh_key_value, key_value_page_store, prefix_len, page_table, context_len):
    tp = lax.axis_size("tp")
    store, fresh = key_value_page_store[0], fresh_key_value[0]
    z = Sizes(tp, store.shape, fresh.shape, queries.shape[1:], page_table.shape)

    def chunk_for(device):
        head = device * z.kv_heads // tp
        pages = lax.dynamic_index_in_dim(store, head, axis=2, keepdims=False)
        new = lax.dynamic_index_in_dim(fresh, head, axis=2, keepdims=False).transpose(1, 0, 2)
        new = jnp.pad(new, ((0, 0), (0, z.new_pad - z.new_rows), (0, 0)))
        return jnp.concatenate([pages.reshape((-1, z.head_dim)), new.reshape((-1, z.head_dim))])

    order = [tp - 2] + list(range(1, tp - 2)) + [tp - 1]
    early, late = [0] + order[: tp // 2 - 1], order[tp // 2 - 1 :]
    chunks = {0: chunk_for(lax.axis_index("tp"))}
    for d in order:
        chunks[d] = lax.ppermute(chunk_for(z.target(d)), "tp", z.pairs(d))
    inputs = (prefix_len, page_table.T, context_len)
    return attend(z, inputs, queries[0], chunks, early, late)[None]


def solution(mesh):
    placed = (
        P(("pairs", "section"), None, "tp"),
        P(("pairs", "section"), "tp", None, None, None),
        P(("pairs", "section"), "tp", None, None, None, None),
        P("pairs"),
        P("pairs", None),
        P("pairs"),
    )
    return jax.shard_map(
        body,
        mesh=mesh,
        in_specs=placed,
        out_specs=P(("pairs", "section"), None, "tp"),
        check_vma=False,
    )
```

```python
import functools
import math

import jax
import jax.numpy as jnp
from jax import lax
from jax.experimental import pallas as pl
from jax.experimental.pallas import tpu as pltpu
from jax.sharding import PartitionSpec as P

FIN_DEV = 1
ROW_TILE = 16
LANES = 128
BLOCK_BATCH = 4
MASKED = -1e30
LOG2_E = 1.4426950408889634


def round_up(value, multiple):
    return -(-value // multiple) * multiple


class Sizes:
    def __init__(self, tp, store, fresh, queries, page_table):
        self.tp = tp
        self.pages_here, _, self.kv_heads, self.page, self.head_dim = store
        self.prefix_pages = self.pages_here - FIN_DEV
        self.per_device = self.pages_here + FIN_DEV
        self.new_rows = fresh[0]
        self.new_pad = round_up(self.new_rows, ROW_TILE)
        self.new_keys = tp * self.new_pad
        self.heads = queries[1] // self.head_dim
        self.row_count = queries[0]
        self.dec_rows, self.max_entries = page_table
        self.steps = self.row_count // self.dec_rows
        self.slots = tp * self.per_device
        self.scale = LOG2_E / math.sqrt(self.head_dim)
        self.new_at = self.pages_here * 2 * self.page
        self.prefill_tiles = round_up(self.heads * self.row_count, LANES) // LANES
        self.row_width = round_up(self.steps * self.heads, LANES)
        self.row_tiles = self.row_width // LANES
        self.decode_tiles = self.dec_rows * self.row_tiles
        self.tiles = max(self.prefill_tiles, self.decode_tiles)
        self.chunk_rows = self.new_at + 2 * self.new_pad
        self.owner_at = 1
        self.valid_at = 1 + self.slots

    def source(self, d):
        return lax.rem(lax.axis_index("tp") + self.tp - d, self.tp)

    def target(self, d):
        return lax.rem(lax.axis_index("tp") + d, self.tp)

    def pairs(self, d):
        return [(i, (i + d) % self.tp) for i in range(self.tp)]


def score(keys, queries):
    return jnp.dot(keys, queries, preferred_element_type=jnp.float32)


def soften(scores, values, scale):
    highest = jnp.max(scores, axis=0, keepdims=True)
    raw = jnp.exp2((scores - highest) * scale)
    total = jnp.sum(raw, axis=0, keepdims=True)
    summed = lax.dot_general(
        values,
        raw.astype(values.dtype),
        (((0,), (0,)), ((), ())),
        preferred_element_type=jnp.float32,
    )
    return summed, highest, total


def merge(first, second, scale):
    highest = jnp.maximum(first[1], second[1])
    keep = jnp.exp2((first[1] - highest) * scale)
    add = jnp.exp2((second[1] - highest) * scale)
    return (
        first[0] * keep + second[0] * add,
        highest,
        first[2] * keep + second[2] * add,
    )


def read(state, tile):
    return tuple(ref[tile] for ref in state)


def write(state, tile, part):
    for ref, value in zip(state, part):
        ref[tile] = value


def settle(part):
    return (part[0] * (1.0 / part[2])).T


def key_rows(z, count):
    return lax.broadcasted_iota(jnp.int32, (count, LANES), 0)


def add_pages(z, pages, plan_ref, queries_ref, state):
    slot = key_rows(z, z.page)
    for start in range(0, len(pages), BLOCK_BATCH):
        parts = []
        for ref, at, number in pages[start : start + BLOCK_BATCH]:
            visible = slot < plan_ref[z.valid_at + number]
            keys, values = ref[at : at + z.page, :], ref[at + z.page : at + 2 * z.page, :]
            for i in range(z.row_tiles):
                tile = plan_ref[z.owner_at + number] * z.row_tiles + i
                scores = jnp.where(visible, score(keys, queries_ref[tile]), MASKED)
                parts.append((tile, soften(scores, values, z.scale)))
        for tile, part in parts:
            write(state, tile, merge(read(state, tile), part, z.scale))


def prefix_visible(z, plan_ref, shifts):
    slot = key_rows(z, z.page)
    return [
        slot < plan_ref[0] - (z.source(d) * z.prefix_pages + q) * z.page
        for d in shifts
        for q in range(z.prefix_pages)
    ]


def prefix_rows(z, chunks, shifts, which):
    return [
        chunks[d][(2 * q + which) * z.page : (2 * q + which + 1) * z.page, :]
        for d in shifts
        for q in range(z.prefix_pages)
    ]


def new_rows(z, new_ref, chunks, which):
    sources = [(new_ref, at) for at in range(0, new_ref.shape[0], 2 * z.new_pad)]
    sources += [(chunk, z.new_at) for chunk in chunks]
    rows = [pl.ds(at + which * z.new_pad, z.new_pad) for _, at in sources]
    return [ref[span, :] for (ref, _), span in zip(sources, rows)]


def new_index(z, shifts):
    within = key_rows(z, z.new_pad)
    none = jnp.full_like(within, z.row_count)
    return jnp.concatenate(
        [
            jnp.where(within < z.new_rows, z.source(d) * z.new_rows + within, none)
            for d in shifts
        ],
        axis=0,
    )


def local_pages(z, chunks, shifts):
    return [
        (chunks[d], 2 * q * z.page, z.source(d) * z.per_device + q)
        for d in shifts
        for q in range(z.pages_here)
    ]


def landed_pages(z, places, shifts):
    return [
        (ref, at + 2 * q * z.page, z.source(d) * z.per_device + z.pages_here + q)
        for (ref, at), d in zip(places, shifts)
        for q in range(FIN_DEV)
    ]


def on_side(side):
    return pl.when(lax.axis_index("section") == side)


def first_kernel(
    z, shifts, prefix_ref, table_ref, context_ref, prefill_ref, decode_ref, *refs
):
    chunks, refs = dict(zip(shifts, refs)), refs[len(shifts) :]
    plan_ref, packed_ref, new_ref, state = refs[0], refs[1], refs[2], refs[3:]
    first, last = z.prefix_pages * 2 * z.page, z.new_at
    for i, d in enumerate(shifts):
        packed_ref[i * (last - first) : (i + 1) * (last - first), :] = chunks[d][first:last, :]
        new_ref[i * 2 * z.new_pad : (i + 1) * 2 * z.new_pad, :] = chunks[d][z.new_at :, :]

    def forget(n, carry):
        plan_ref[z.owner_at + n] = 0
        plan_ref[z.valid_at + n] = 0
        return carry

    def note(r, carry):
        length = context_ref[r]
        for m in range(z.max_entries):

            @pl.when(m * z.page < length)
            def used():
                number = jnp.clip(table_ref[m, r], 0, z.slots - 1)
                plan_ref[z.owner_at + number] = r
                plan_ref[z.valid_at + number] = jnp.minimum(length - m * z.page, z.page)

        return carry

    plan_ref[0] = prefix_ref[0]
    lax.fori_loop(0, z.slots, forget, 0)
    lax.fori_loop(0, z.dec_rows, note, 0)

    @on_side(0)
    def prefill():
        visible = jnp.concatenate(prefix_visible(z, plan_ref, shifts), axis=0)
        keys = jnp.concatenate(prefix_rows(z, chunks, shifts, 0), axis=0)
        values = jnp.concatenate(prefix_rows(z, chunks, shifts, 1), axis=0)
        for tile in range(z.prefill_tiles):
            scores = jnp.where(visible, score(keys, prefill_ref[tile]), MASKED)
            write(state, tile, soften(scores, values, z.scale))

    @on_side(1)
    def decode():
        state[0][...] = jnp.zeros_like(state[0])
        state[1][...] = jnp.full_like(state[1], MASKED)
        state[2][...] = jnp.zeros_like(state[2])
        pages = local_pages(z, chunks, shifts)
        add_pages(z, pages, plan_ref, decode_ref, state)


def second_kernel(z, groups, stored_plan_ref, prefill_ref, decode_ref, *refs):
    shifts = groups[1]
    refs, (plan_ref, plan_sem) = refs[:-2], refs[-2:]
    plan_copy = pltpu.make_async_copy(stored_plan_ref, plan_ref, plan_sem)
    plan_copy.start()
    before, new_ref, refs = refs[:3], refs[3], refs[4:]
    late, refs = refs[: len(shifts)], refs[len(shifts) :]
    state, (out_ref, held_ref, sems) = refs[:3], refs[3:]
    chunks = dict(zip(shifts, late))
    index = new_index(z, groups[0] + groups[1])
    column = lax.broadcasted_iota(jnp.int32, (1, LANES), 1)
    new_keys = jnp.concatenate(new_rows(z, new_ref, late, 0), axis=0)

    @on_side(0)
    def prefill():
        plan_copy.wait()
        visible = jnp.concatenate(prefix_visible(z, plan_ref, shifts), axis=0)
        keys = prefix_rows(z, chunks, shifts, 0)
        cached = len(keys) * z.page
        keys = jnp.concatenate(keys + new_rows(z, new_ref, late, 0), axis=0)
        values = prefix_rows(z, chunks, shifts, 1) + new_rows(z, new_ref, late, 1)
        values = jnp.concatenate(values, axis=0)
        copies = []
        for tile in range(z.prefill_tiles):
            query = lax.rem(column + tile * LANES, z.row_count)
            scores = score(keys, prefill_ref[tile])
            scores = jnp.concatenate(
                [
                    jnp.where(visible, scores[:cached], MASKED),
                    jnp.where(index <= query, scores[cached:], MASKED),
                ],
                axis=0,
            )
            part = merge(read(before, tile), soften(scores, values, z.scale), z.scale)
            held_ref[tile * LANES : (tile + 1) * LANES, :] = settle(part).astype(held_ref.dtype)
            while len(copies) < min((tile + 1) * LANES // z.row_count, z.heads):
                h = len(copies)
                source = held_ref.at[pl.ds(h * z.row_count, z.row_count)]
                target = out_ref.at[:, pl.ds(h * z.head_dim, z.head_dim)]
                copies.append(pltpu.make_async_copy(source, target, sems.at[h]))
                copies[-1].start()
        for copy in copies:
            copy.wait()

    @on_side(1)
    def decode():
        owner = lax.rem(index, z.dec_rows)
        owner = jnp.where(index < z.row_count, owner, -1)
        step = index // z.dec_rows
        new_values = jnp.concatenate(new_rows(z, new_ref, late, 1), axis=0)
        for tile in range(z.decode_tiles):
            row, i = divmod(tile, z.row_tiles)
            query = (column + i * LANES) // z.heads
            visible = (owner == row) & (step <= query)
            scores = jnp.where(visible, score(new_keys, decode_ref[tile]), MASKED)
            part = soften(scores, new_values, z.scale)
            write(state, tile, merge(read(before, tile), part, z.scale))
        pages = local_pages(z, chunks, shifts)
        plan_copy.wait()
        add_pages(z, pages, plan_ref, decode_ref, state)


def last_kernel(z, groups, stored_plan_ref, decode_ref, early_ref, *refs):
    refs, (plan_ref, plan_sem) = refs[:-2], refs[-2:]
    plan_copy = pltpu.make_async_copy(stored_plan_ref, plan_ref, plan_sem)
    plan_copy.start()
    late, refs = refs[: len(groups[1])], refs[len(groups[1]) :]
    before, out_ref, refs = refs[:3], refs[4], refs[5:]
    state, (held_ref, rows_ref, sems) = refs[:3], refs[3:]

    @on_side(0)
    def prefill():
        plan_copy.wait()

    @on_side(1)
    def decode():
        for ref, value in zip(state, before):
            ref[...] = value[...]
        plan_copy.wait()
        places = [(early_ref, i * FIN_DEV * 2 * z.page) for i in range(len(groups[0]))]
        places += [(ref, z.prefix_pages * 2 * z.page) for ref in late]
        pages = landed_pages(z, places, groups[0] + groups[1])
        add_pages(z, pages, plan_ref, decode_ref, state)
        for tile in range(z.decode_tiles):
            held_ref[tile * LANES : (tile + 1) * LANES, :] = settle(read(state, tile))
        copies = []
        for s in range(z.steps):
            span = pl.ds(s * z.dec_rows, z.dec_rows)
            for h in range(z.heads):
                rows = pl.ds(s * z.heads + h, z.dec_rows, stride=z.row_width)
                rows_ref[span, h * z.head_dim : (h + 1) * z.head_dim] = held_ref[rows, :].astype(
                    rows_ref.dtype
                )
            copies.append(
                pltpu.make_async_copy(rows_ref.at[span], out_ref.at[span], sems.at[s])
            )
            copies[-1].start()
        for copy in copies:
            copy.wait()


def call(kernel, z, shifts, name, keys, operands, outputs, scratch=(), aliases=None):
    spaces = {"smem": pltpu.SMEM, "vmem": pltpu.VMEM, "any": pl.ANY}
    spec = {key: pl.BlockSpec(memory_space=space) for key, space in spaces.items()}
    return pl.pallas_call(
        functools.partial(kernel, z, shifts),
        out_shape=[shape for _, shape in outputs],
        in_specs=[spec[key] for key, _ in operands],
        out_specs=[spec[key] for key, _ in outputs],
        scratch_shapes=list(scratch),
        input_output_aliases=aliases or {},
        compiler_params=pltpu.CompilerParams(vmem_limit_bytes=16 * 1024 * 1024),
        cost_estimate=pl.CostEstimate(
            flops=4 * z.tiles * LANES * keys * z.head_dim,
            bytes_accessed=2 * z.tiles * LANES * z.head_dim * 8,
            transcendentals=z.tiles * LANES * keys,
        ),
        name=name,
    )(*[value for _, value in operands])


def query_tiles(z, queries):
    by_head = queries.reshape((z.row_count, z.heads, z.head_dim)).transpose(1, 0, 2)
    by_head = by_head.reshape((-1, z.head_dim))
    spare = z.prefill_tiles * LANES - by_head.shape[0]
    by_head = jnp.pad(by_head, ((0, spare), (0, 0)))
    by_row = queries.reshape((z.steps, z.dec_rows, z.heads, z.head_dim)).transpose(1, 0, 2, 3)
    by_row = by_row.reshape((z.dec_rows, z.steps * z.heads, z.head_dim))
    by_row = jnp.pad(by_row, ((0, 0), (0, z.row_width - z.steps * z.heads), (0, 0)))
    return (
        by_head.reshape((z.prefill_tiles, LANES, z.head_dim)).transpose(0, 2, 1),
        by_row.reshape((z.decode_tiles, LANES, z.head_dim)).transpose(0, 2, 1),
    )


def hand_over(pages):
    return lax.ppermute(pages, "section", [(0, 1), (1, 0)])


def attend(z, inputs, queries, chunks, early, late):
    prefill, decode = query_tiles(z, queries)

    def shaped(space, shape, dtype):
        return (space, jax.ShapeDtypeStruct(shape, dtype))

    state = [
        shaped("vmem", (z.tiles, rows, LANES), jnp.float32) for rows in (z.head_dim, 1, 1)
    ]
    out = shaped("any", queries.shape, queries.dtype)
    plan, packed, new, *first = call(
        first_kernel,
        z,
        early,
        "early_pages",
        len(early) * z.page,
        [("smem", value) for value in inputs]
        + [("vmem", value) for value in (prefill, decode)]
        + [("vmem", chunks[d]) for d in early],
        [shaped("smem", (1 + 2 * z.slots,), jnp.int32)]
        + [
            shaped("vmem", (len(early) * rows, z.head_dim), queries.dtype)
            for rows in (FIN_DEV * 2 * z.page, 2 * z.new_pad)
        ]
        + state,
    )
    *waiting, plan = lax.optimization_barrier((*[chunks[d] for d in early + late], plan))
    landed = [hand_over(packed)] + [hand_over(chunk) for chunk in waiting[len(early) :]]
    *second, done = call(
        second_kernel,
        z,
        (early, late),
        "late_pages",
        len(late) * z.page + z.new_keys,
        [("any", plan)]
        + [("vmem", value) for value in (prefill, decode, *first, new)]
        + [("vmem", chunks[d]) for d in late],
        state + [out],
        [
            pltpu.VMEM((z.prefill_tiles * LANES, z.head_dim), queries.dtype),
            pltpu.SemaphoreType.DMA((z.heads,)),
            pltpu.SMEM(plan.shape, plan.dtype),
            pltpu.SemaphoreType.DMA,
        ],
    )
    operands = [("any", plan)]
    operands += [("vmem", value) for value in (decode, *landed, *second)]
    (result,) = call(
        last_kernel,
        z,
        (early, late),
        "landed_pages",
        z.page,
        operands + [("any", done)],
        [out],
        [pltpu.VMEM(shape.shape, shape.dtype) for _, shape in state]
        + [
            pltpu.VMEM((z.decode_tiles * LANES, z.head_dim), jnp.float32),
            pltpu.VMEM(queries.shape, queries.dtype),
            pltpu.SemaphoreType.DMA((z.steps,)),
            pltpu.SMEM(plan.shape, plan.dtype),
            pltpu.SemaphoreType.DMA,
        ],
        {len(operands): 0},
    )
    return result


def body(queries, fresh_key_value, key_value_page_store, prefix_len, page_table, context_len):
    tp = lax.axis_size("tp")
    store, fresh = key_value_page_store[0], fresh_key_value[0]
    z = Sizes(tp, store.shape, fresh.shape, queries.shape[1:], page_table.shape)

    def chunk_for(device):
        head = device * z.kv_heads // tp
        pages = lax.dynamic_index_in_dim(store, head, axis=2, keepdims=False)
        new = lax.dynamic_index_in_dim(fresh, head, axis=2, keepdims=False).transpose(1, 0, 2)
        new = jnp.pad(new, ((0, 0), (0, z.new_pad - z.new_rows), (0, 0)))
        return jnp.concatenate([pages.reshape((-1, z.head_dim)), new.reshape((-1, z.head_dim))])

    order = [tp - 2] + list(range(1, tp - 2)) + [tp - 1]
    early, late = [0] + order[: tp // 2 - 1], order[tp // 2 - 1 :]
    chunks = {0: chunk_for(lax.axis_index("tp"))}
    for d in order:
        chunks[d] = lax.ppermute(chunk_for(z.target(d)), "tp", z.pairs(d))
    inputs = (prefix_len, page_table.T, context_len)
    return attend(z, inputs, queries[0], chunks, early, late)[None]


def solution(mesh):
    placed = (
        P(("pairs", "section"), None, "tp"),
        P(("pairs", "section"), "tp", None, None, None),
        P(("pairs", "section"), "tp", None, None, None, None),
        P("pairs"),
        P("pairs", None),
        P("pairs"),
    )
    return jax.shard_map(
        body,
        mesh=mesh,
        in_specs=placed,
        out_specs=P(("pairs", "section"), None, "tp"),
        check_vma=False,
    )
```

```python
import functools
import math

import jax
import jax.numpy as jnp
from jax import lax
from jax.experimental import pallas as pl
from jax.experimental.pallas import tpu as pltpu
from jax.sharding import PartitionSpec as P

FIN_DEV = 1
ROW_TILE = 16
LANES = 128
BLOCK_BATCH = 4
MASKED = -1e30
LOG2_E = 1.4426950408889634


def round_up(value, multiple):
    return -(-value // multiple) * multiple


class Sizes:
    def __init__(self, tp, store, fresh, queries, page_table):
        self.tp = tp
        self.pages_here, _, self.kv_heads, self.page, self.head_dim = store
        self.prefix_pages = self.pages_here - FIN_DEV
        self.per_device = self.pages_here + FIN_DEV
        self.new_rows = fresh[0]
        self.new_pad = round_up(self.new_rows, ROW_TILE)
        self.new_keys = tp * self.new_pad
        self.heads = queries[1] // self.head_dim
        self.row_count = queries[0]
        self.dec_rows, self.max_entries = page_table
        self.steps = self.row_count // self.dec_rows
        self.slots = tp * self.per_device
        self.scale = LOG2_E / math.sqrt(self.head_dim)
        self.new_at = self.pages_here * 2 * self.page
        self.prefill_tiles = round_up(self.heads * self.row_count, LANES) // LANES
        self.row_width = round_up(self.steps * self.heads, LANES)
        self.row_tiles = self.row_width // LANES
        self.decode_tiles = self.dec_rows * self.row_tiles
        self.tiles = max(self.prefill_tiles, self.decode_tiles)
        self.chunk_rows = self.new_at + 2 * self.new_pad
        self.owner_at = 1
        self.valid_at = 1 + self.slots

    def source(self, d):
        return lax.rem(lax.axis_index("tp") + self.tp - d, self.tp)

    def target(self, d):
        return lax.rem(lax.axis_index("tp") + d, self.tp)

    def pairs(self, d):
        return [(i, (i + d) % self.tp) for i in range(self.tp)]


def score(keys, queries):
    return jnp.dot(keys, queries, preferred_element_type=jnp.float32)


def soften(scores, values, scale):
    highest = jnp.max(scores, axis=0, keepdims=True)
    raw = jnp.exp2((scores - highest) * scale)
    total = jnp.sum(raw, axis=0, keepdims=True)
    summed = lax.dot_general(
        values,
        raw.astype(values.dtype),
        (((0,), (0,)), ((), ())),
        preferred_element_type=jnp.float32,
    )
    return summed, highest, total


def merge(first, second, scale):
    highest = jnp.maximum(first[1], second[1])
    keep = jnp.exp2((first[1] - highest) * scale)
    add = jnp.exp2((second[1] - highest) * scale)
    return (
        first[0] * keep + second[0] * add,
        highest,
        first[2] * keep + second[2] * add,
    )


def read(state, tile):
    return tuple(ref[tile] for ref in state)


def write(state, tile, part):
    for ref, value in zip(state, part):
        ref[tile] = value


def settle(part):
    return (part[0] * (1.0 / part[2])).T


def key_rows(z, count):
    return lax.broadcasted_iota(jnp.int32, (count, LANES), 0)


def add_pages(z, pages, plan_ref, queries_ref, state):
    slot = key_rows(z, z.page)
    for start in range(0, len(pages), BLOCK_BATCH):
        parts = []
        for ref, at, number in pages[start : start + BLOCK_BATCH]:
            visible = slot < plan_ref[z.valid_at + number]
            keys, values = ref[at : at + z.page, :], ref[at + z.page : at + 2 * z.page, :]
            for i in range(z.row_tiles):
                tile = plan_ref[z.owner_at + number] * z.row_tiles + i
                scores = jnp.where(visible, score(keys, queries_ref[tile]), MASKED)
                parts.append((tile, soften(scores, values, z.scale)))
        for tile, part in parts:
            write(state, tile, merge(read(state, tile), part, z.scale))


def prefix_visible(z, plan_ref, shifts):
    slot = key_rows(z, z.page)
    return [
        slot < plan_ref[0] - (z.source(d) * z.prefix_pages + q) * z.page
        for d in shifts
        for q in range(z.prefix_pages)
    ]


def prefix_rows(z, chunks, shifts, which):
    return [
        chunks[d][(2 * q + which) * z.page : (2 * q + which + 1) * z.page, :]
        for d in shifts
        for q in range(z.prefix_pages)
    ]


def new_rows(z, new_ref, chunks, which):
    sources = [(new_ref, at) for at in range(0, new_ref.shape[0], 2 * z.new_pad)]
    sources += [(chunk, z.new_at) for chunk in chunks]
    rows = [pl.ds(at + which * z.new_pad, z.new_pad) for _, at in sources]
    return [ref[span, :] for (ref, _), span in zip(sources, rows)]


def new_index(z, shifts):
    within = key_rows(z, z.new_pad)
    none = jnp.full_like(within, z.row_count)
    return jnp.concatenate(
        [
            jnp.where(within < z.new_rows, z.source(d) * z.new_rows + within, none)
            for d in shifts
        ],
        axis=0,
    )


def local_pages(z, chunks, shifts):
    return [
        (chunks[d], 2 * q * z.page, z.source(d) * z.per_device + q)
        for d in shifts
        for q in range(z.pages_here)
    ]


def landed_pages(z, places, shifts):
    return [
        (ref, at + 2 * q * z.page, z.source(d) * z.per_device + z.pages_here + q)
        for (ref, at), d in zip(places, shifts)
        for q in range(FIN_DEV)
    ]


def on_side(side):
    return pl.when(lax.axis_index("section") == side)


def first_kernel(
    z, shifts, prefix_ref, table_ref, context_ref, prefill_ref, decode_ref, *refs
):
    chunks, refs = dict(zip(shifts, refs)), refs[len(shifts) :]
    plan_ref, packed_ref, new_ref, state = refs[0], refs[1], refs[2], refs[3:]
    first, last = z.prefix_pages * 2 * z.page, z.new_at
    for i, d in enumerate(shifts):
        packed_ref[i * (last - first) : (i + 1) * (last - first), :] = chunks[d][first:last, :]
        new_ref[i * 2 * z.new_pad : (i + 1) * 2 * z.new_pad, :] = chunks[d][z.new_at :, :]

    def forget(n, carry):
        plan_ref[z.owner_at + n] = 0
        plan_ref[z.valid_at + n] = 0
        return carry

    def note(r, carry):
        length = context_ref[r]
        for m in range(z.max_entries):

            @pl.when(m * z.page < length)
            def used():
                number = jnp.clip(table_ref[m, r], 0, z.slots - 1)
                plan_ref[z.owner_at + number] = r
                plan_ref[z.valid_at + number] = jnp.minimum(length - m * z.page, z.page)

        return carry

    plan_ref[0] = prefix_ref[0]
    lax.fori_loop(0, z.slots, forget, 0)
    lax.fori_loop(0, z.dec_rows, note, 0)

    @on_side(0)
    def prefill():
        visible = jnp.concatenate(prefix_visible(z, plan_ref, shifts), axis=0)
        keys = jnp.concatenate(prefix_rows(z, chunks, shifts, 0), axis=0)
        values = jnp.concatenate(prefix_rows(z, chunks, shifts, 1), axis=0)
        for tile in range(z.prefill_tiles):
            scores = jnp.where(visible, score(keys, prefill_ref[tile]), MASKED)
            write(state, tile, soften(scores, values, z.scale))

    @on_side(1)
    def decode():
        state[0][...] = jnp.zeros_like(state[0])
        state[1][...] = jnp.full_like(state[1], MASKED)
        state[2][...] = jnp.zeros_like(state[2])
        pages = local_pages(z, chunks, shifts)
        add_pages(z, pages, plan_ref, decode_ref, state)


def second_kernel(z, groups, stored_plan_ref, prefill_ref, decode_ref, *refs):
    shifts = groups[1]
    refs, (plan_ref, plan_sem) = refs[:-2], refs[-2:]
    plan_copy = pltpu.make_async_copy(stored_plan_ref, plan_ref, plan_sem)
    plan_copy.start()
    before, new_ref, refs = refs[:3], refs[3], refs[4:]
    late, refs = refs[: len(shifts)], refs[len(shifts) :]
    state, (out_ref, held_ref, sems) = refs[:3], refs[3:]
    chunks = dict(zip(shifts, late))
    index = new_index(z, groups[0] + groups[1])
    column = lax.broadcasted_iota(jnp.int32, (1, LANES), 1)
    new_keys = jnp.concatenate(new_rows(z, new_ref, late, 0), axis=0)

    @on_side(0)
    def prefill():
        plan_copy.wait()
        visible = jnp.concatenate(prefix_visible(z, plan_ref, shifts), axis=0)
        keys = prefix_rows(z, chunks, shifts, 0)
        cached = len(keys) * z.page
        keys = jnp.concatenate(keys + new_rows(z, new_ref, late, 0), axis=0)
        values = prefix_rows(z, chunks, shifts, 1) + new_rows(z, new_ref, late, 1)
        values = jnp.concatenate(values, axis=0)
        copies = []
        for tile in range(z.prefill_tiles):
            query = lax.rem(column + tile * LANES, z.row_count)
            scores = score(keys, prefill_ref[tile])
            scores = jnp.concatenate(
                [
                    jnp.where(visible, scores[:cached], MASKED),
                    jnp.where(index <= query, scores[cached:], MASKED),
                ],
                axis=0,
            )
            part = merge(read(before, tile), soften(scores, values, z.scale), z.scale)
            held_ref[tile * LANES : (tile + 1) * LANES, :] = settle(part).astype(held_ref.dtype)
            while len(copies) < min((tile + 1) * LANES // z.row_count, z.heads):
                h = len(copies)
                source = held_ref.at[pl.ds(h * z.row_count, z.row_count)]
                target = out_ref.at[:, pl.ds(h * z.head_dim, z.head_dim)]
                copies.append(pltpu.make_async_copy(source, target, sems.at[h]))
                copies[-1].start()
        for copy in copies:
            copy.wait()

    @on_side(1)
    def decode():
        owner = lax.rem(index, z.dec_rows)
        owner = jnp.where(index < z.row_count, owner, -1)
        step = index // z.dec_rows
        new_values = jnp.concatenate(new_rows(z, new_ref, late, 1), axis=0)
        for tile in range(z.decode_tiles):
            row, i = divmod(tile, z.row_tiles)
            query = (column + i * LANES) // z.heads
            visible = (owner == row) & (step <= query)
            scores = jnp.where(visible, score(new_keys, decode_ref[tile]), MASKED)
            part = soften(scores, new_values, z.scale)
            write(state, tile, merge(read(before, tile), part, z.scale))
        pages = local_pages(z, chunks, shifts)
        plan_copy.wait()
        add_pages(z, pages, plan_ref, decode_ref, state)


def last_kernel(z, groups, stored_plan_ref, decode_ref, early_ref, *refs):
    refs, (plan_ref, plan_sem) = refs[:-2], refs[-2:]
    plan_copy = pltpu.make_async_copy(stored_plan_ref, plan_ref, plan_sem)
    plan_copy.start()
    late, refs = refs[: len(groups[1])], refs[len(groups[1]) :]
    before, out_ref, refs = refs[:3], refs[4], refs[5:]
    state, (held_ref, rows_ref, sems) = refs[:3], refs[3:]

    @on_side(0)
    def prefill():
        plan_copy.wait()

    @on_side(1)
    def decode():
        for ref, value in zip(state, before):
            ref[...] = value[...]
        plan_copy.wait()
        places = [(early_ref, i * FIN_DEV * 2 * z.page) for i in range(len(groups[0]))]
        places += [(ref, z.prefix_pages * 2 * z.page) for ref in late]
        pages = landed_pages(z, places, groups[0] + groups[1])
        add_pages(z, pages, plan_ref, decode_ref, state)
        for tile in range(z.decode_tiles):
            held_ref[tile * LANES : (tile + 1) * LANES, :] = settle(read(state, tile))
        copies = []
        for s in range(z.steps):
            span = pl.ds(s * z.dec_rows, z.dec_rows)
            for h in range(z.heads):
                rows = pl.ds(s * z.heads + h, z.dec_rows, stride=z.row_width)
                rows_ref[span, h * z.head_dim : (h + 1) * z.head_dim] = held_ref[rows, :].astype(
                    rows_ref.dtype
                )
            copies.append(
                pltpu.make_async_copy(rows_ref.at[span], out_ref.at[span], sems.at[s])
            )
            copies[-1].start()
        for copy in copies:
            copy.wait()


def call(kernel, z, shifts, name, keys, operands, outputs, scratch=(), aliases=None):
    spaces = {"smem": pltpu.SMEM, "vmem": pltpu.VMEM, "any": pl.ANY}
    spec = {key: pl.BlockSpec(memory_space=space) for key, space in spaces.items()}
    return pl.pallas_call(
        functools.partial(kernel, z, shifts),
        out_shape=[shape for _, shape in outputs],
        in_specs=[spec[key] for key, _ in operands],
        out_specs=[spec[key] for key, _ in outputs],
        scratch_shapes=list(scratch),
        input_output_aliases=aliases or {},
        compiler_params=pltpu.CompilerParams(vmem_limit_bytes=16 * 1024 * 1024),
        cost_estimate=pl.CostEstimate(
            flops=4 * z.tiles * LANES * keys * z.head_dim,
            bytes_accessed=2 * z.tiles * LANES * z.head_dim * 8,
            transcendentals=z.tiles * LANES * keys,
        ),
        name=name,
    )(*[value for _, value in operands])


def query_tiles(z, queries):
    by_head = queries.reshape((z.row_count, z.heads, z.head_dim)).transpose(1, 0, 2)
    by_head = by_head.reshape((-1, z.head_dim))
    spare = z.prefill_tiles * LANES - by_head.shape[0]
    by_head = jnp.pad(by_head, ((0, spare), (0, 0)))
    by_row = queries.reshape((z.steps, z.dec_rows, z.heads, z.head_dim)).transpose(1, 0, 2, 3)
    by_row = by_row.reshape((z.dec_rows, z.steps * z.heads, z.head_dim))
    by_row = jnp.pad(by_row, ((0, 0), (0, z.row_width - z.steps * z.heads), (0, 0)))
    return (
        by_head.reshape((z.prefill_tiles, LANES, z.head_dim)).transpose(0, 2, 1),
        by_row.reshape((z.decode_tiles, LANES, z.head_dim)).transpose(0, 2, 1),
    )


def hand_over(pages):
    return lax.ppermute(pages, "section", [(0, 1), (1, 0)])


def attend(z, inputs, queries, chunks, early, late):
    prefill, decode = query_tiles(z, queries)

    def shaped(space, shape, dtype):
        return (space, jax.ShapeDtypeStruct(shape, dtype))

    state = [
        shaped("vmem", (z.tiles, rows, LANES), jnp.float32) for rows in (z.head_dim, 1, 1)
    ]
    out = shaped("any", queries.shape, queries.dtype)
    plan, packed, new, *first = call(
        first_kernel,
        z,
        early,
        "early_pages",
        len(early) * z.page,
        [("smem", value) for value in inputs]
        + [("vmem", value) for value in (prefill, decode)]
        + [("vmem", chunks[d]) for d in early],
        [shaped("smem", (1 + 2 * z.slots,), jnp.int32)]
        + [
            shaped("vmem", (len(early) * rows, z.head_dim), queries.dtype)
            for rows in (FIN_DEV * 2 * z.page, 2 * z.new_pad)
        ]
        + state,
    )
    *waiting, plan = lax.optimization_barrier((*[chunks[d] for d in early + late], plan))
    landed = [hand_over(packed)] + [hand_over(chunk) for chunk in waiting[len(early) :]]
    *second, done = call(
        second_kernel,
        z,
        (early, late),
        "late_pages",
        len(late) * z.page + z.new_keys,
        [("any", plan)]
        + [("vmem", value) for value in (prefill, decode, *first, new)]
        + [("vmem", chunks[d]) for d in late],
        state + [out],
        [
            pltpu.VMEM((z.prefill_tiles * LANES, z.head_dim), queries.dtype),
            pltpu.SemaphoreType.DMA((z.heads,)),
            pltpu.SMEM(plan.shape, plan.dtype),
            pltpu.SemaphoreType.DMA,
        ],
    )
    operands = [("any", plan)]
    operands += [("vmem", value) for value in (decode, *landed, *second)]
    (result,) = call(
        last_kernel,
        z,
        (early, late),
        "landed_pages",
        z.page,
        operands + [("any", done)],
        [out],
        [pltpu.VMEM(shape.shape, shape.dtype) for _, shape in state]
        + [
            pltpu.VMEM((z.decode_tiles * LANES + z.row_width, z.head_dim), jnp.float32),
            pltpu.VMEM(queries.shape, queries.dtype),
            pltpu.SemaphoreType.DMA((z.steps,)),
            pltpu.SMEM(plan.shape, plan.dtype),
            pltpu.SemaphoreType.DMA,
        ],
        {len(operands): 0},
    )
    return result


def body(queries, fresh_key_value, key_value_page_store, prefix_len, page_table, context_len):
    tp = lax.axis_size("tp")
    store, fresh = key_value_page_store[0], fresh_key_value[0]
    z = Sizes(tp, store.shape, fresh.shape, queries.shape[1:], page_table.shape)

    def chunk_for(device):
        head = device * z.kv_heads // tp
        pages = lax.dynamic_index_in_dim(store, head, axis=2, keepdims=False)
        new = lax.dynamic_index_in_dim(fresh, head, axis=2, keepdims=False).transpose(1, 0, 2)
        new = jnp.pad(new, ((0, 0), (0, z.new_pad - z.new_rows), (0, 0)))
        return jnp.concatenate([pages.reshape((-1, z.head_dim)), new.reshape((-1, z.head_dim))])

    order = [2, tp - 2, 1] + list(range(3, tp - 2)) + [tp - 1]
    early, late = [0] + order[: tp // 2 - 1], order[tp // 2 - 1 :]
    chunks = {0: chunk_for(lax.axis_index("tp"))}
    for d in order:
        chunks[d] = lax.ppermute(chunk_for(z.target(d)), "tp", z.pairs(d))
    inputs = (prefix_len, page_table.T, context_len)
    return attend(z, inputs, queries[0], chunks, early, late)[None]


def solution(mesh):
    placed = (
        P(("pairs", "section"), None, "tp"),
        P(("pairs", "section"), "tp", None, None, None),
        P(("pairs", "section"), "tp", None, None, None, None),
        P("pairs"),
        P("pairs", None),
        P("pairs"),
    )
    return jax.shard_map(
        body,
        mesh=mesh,
        in_specs=placed,
        out_specs=P(("pairs", "section"), None, "tp"),
        check_vma=False,
    )
```

```python
import functools
import math

import jax
import jax.numpy as jnp
from jax import lax
from jax.experimental import pallas as pl
from jax.experimental.pallas import tpu as pltpu
from jax.sharding import PartitionSpec as P

FIN_DEV = 1
ROW_TILE = 16
LANES = 128
BLOCK_BATCH = 4
MASKED = -1e30
LOG2_E = 1.4426950408889634


def round_up(value, multiple):
    return -(-value // multiple) * multiple


class Sizes:
    def __init__(self, tp, store, fresh, queries, page_table):
        self.tp = tp
        self.pages_here, _, self.kv_heads, self.page, self.head_dim = store
        self.prefix_pages = self.pages_here - FIN_DEV
        self.per_device = self.pages_here + FIN_DEV
        self.new_rows = fresh[0]
        self.new_pad = round_up(self.new_rows, ROW_TILE)
        self.new_keys = tp * self.new_pad
        self.heads = queries[1] // self.head_dim
        self.row_count = queries[0]
        self.dec_rows, self.max_entries = page_table
        self.steps = self.row_count // self.dec_rows
        self.slots = tp * self.per_device
        self.scale = LOG2_E / math.sqrt(self.head_dim)
        self.new_at = self.pages_here * 2 * self.page
        self.prefill_tiles = round_up(self.heads * self.row_count, LANES) // LANES
        self.row_width = round_up(self.steps * self.heads, LANES)
        self.row_tiles = self.row_width // LANES
        self.decode_tiles = self.dec_rows * self.row_tiles
        self.tiles = max(self.prefill_tiles, self.decode_tiles)
        self.chunk_rows = self.new_at + 2 * self.new_pad
        self.owner_at = 1
        self.valid_at = 1 + self.slots

    def source(self, d):
        return lax.rem(lax.axis_index("tp") + self.tp - d, self.tp)

    def target(self, d):
        return lax.rem(lax.axis_index("tp") + d, self.tp)

    def pairs(self, d):
        return [(i, (i + d) % self.tp) for i in range(self.tp)]


def score(keys, queries):
    return jnp.dot(keys, queries, preferred_element_type=jnp.float32)


def soften(scores, values, scale):
    highest = jnp.max(scores, axis=0, keepdims=True)
    raw = jnp.exp2((scores - highest) * scale)
    total = jnp.sum(raw, axis=0, keepdims=True)
    summed = lax.dot_general(
        values,
        raw.astype(values.dtype),
        (((0,), (0,)), ((), ())),
        preferred_element_type=jnp.float32,
    )
    return summed, highest, total


def merge(first, second, scale):
    highest = jnp.maximum(first[1], second[1])
    keep = jnp.exp2((first[1] - highest) * scale)
    add = jnp.exp2((second[1] - highest) * scale)
    return (
        first[0] * keep + second[0] * add,
        highest,
        first[2] * keep + second[2] * add,
    )


def read(state, tile):
    return tuple(ref[tile] for ref in state)


def write(state, tile, part):
    for ref, value in zip(state, part):
        ref[tile] = value


def settle(part, kind):
    return (part[0] * (1.0 / part[2])).astype(kind).T


def key_rows(z, count):
    return lax.broadcasted_iota(jnp.int32, (count, LANES), 0)


def add_pages(z, pages, plan_ref, queries_ref, state):
    slot = key_rows(z, z.page)
    for start in range(0, len(pages), BLOCK_BATCH):
        parts = []
        for ref, at, number in pages[start : start + BLOCK_BATCH]:
            visible = slot < plan_ref[z.valid_at + number]
            keys, values = ref[at : at + z.page, :], ref[at + z.page : at + 2 * z.page, :]
            for i in range(z.row_tiles):
                tile = plan_ref[z.owner_at + number] * z.row_tiles + i
                scores = jnp.where(visible, score(keys, queries_ref[tile]), MASKED)
                parts.append((tile, soften(scores, values, z.scale)))
        for tile, part in parts:
            write(state, tile, merge(read(state, tile), part, z.scale))


def prefix_visible(z, plan_ref, shifts):
    slot = key_rows(z, z.page)
    return [
        slot < plan_ref[0] - (z.source(d) * z.prefix_pages + q) * z.page
        for d in shifts
        for q in range(z.prefix_pages)
    ]


def prefix_rows(z, chunks, shifts, which):
    return [
        chunks[d][(2 * q + which) * z.page : (2 * q + which + 1) * z.page, :]
        for d in shifts
        for q in range(z.prefix_pages)
    ]


def new_rows(z, new_ref, chunks, which):
    sources = [(new_ref, at) for at in range(0, new_ref.shape[0], 2 * z.new_pad)]
    sources += [(chunk, z.new_at) for chunk in chunks]
    rows = [pl.ds(at + which * z.new_pad, z.new_pad) for _, at in sources]
    return [ref[span, :] for (ref, _), span in zip(sources, rows)]


def new_index(z, shifts):
    within = key_rows(z, z.new_pad)
    none = jnp.full_like(within, z.row_count)
    return jnp.concatenate(
        [
            jnp.where(within < z.new_rows, z.source(d) * z.new_rows + within, none)
            for d in shifts
        ],
        axis=0,
    )


def local_pages(z, chunks, shifts):
    return [
        (chunks[d], 2 * q * z.page, z.source(d) * z.per_device + q)
        for d in shifts
        for q in range(z.pages_here)
    ]


def landed_pages(z, places, shifts):
    return [
        (ref, at + 2 * q * z.page, z.source(d) * z.per_device + z.pages_here + q)
        for (ref, at), d in zip(places, shifts)
        for q in range(FIN_DEV)
    ]


def on_side(side):
    return pl.when(lax.axis_index("section") == side)


def first_kernel(
    z, shifts, prefix_ref, table_ref, context_ref, prefill_ref, decode_ref, *refs
):
    chunks, refs = dict(zip(shifts, refs)), refs[len(shifts) :]
    plan_ref, packed_ref, new_ref, state = refs[0], refs[1], refs[2], refs[3:]
    first, last = z.prefix_pages * 2 * z.page, z.new_at
    for i, d in enumerate(shifts):
        packed_ref[i * (last - first) : (i + 1) * (last - first), :] = chunks[d][first:last, :]
        new_ref[i * 2 * z.new_pad : (i + 1) * 2 * z.new_pad, :] = chunks[d][z.new_at :, :]

    def forget(n, carry):
        plan_ref[z.owner_at + n] = 0
        plan_ref[z.valid_at + n] = 0
        return carry

    def note(r, carry):
        length = context_ref[r]
        for m in range(z.max_entries):

            @pl.when(m * z.page < length)
            def used():
                number = jnp.clip(table_ref[m, r], 0, z.slots - 1)
                plan_ref[z.owner_at + number] = r
                plan_ref[z.valid_at + number] = jnp.minimum(length - m * z.page, z.page)

        return carry

    plan_ref[0] = prefix_ref[0]
    lax.fori_loop(0, z.slots, forget, 0)
    lax.fori_loop(0, z.dec_rows, note, 0)

    @on_side(0)
    def prefill():
        visible = jnp.concatenate(prefix_visible(z, plan_ref, shifts), axis=0)
        keys = jnp.concatenate(prefix_rows(z, chunks, shifts, 0), axis=0)
        values = jnp.concatenate(prefix_rows(z, chunks, shifts, 1), axis=0)
        for tile in range(z.prefill_tiles):
            scores = jnp.where(visible, score(keys, prefill_ref[tile]), MASKED)
            write(state, tile, soften(scores, values, z.scale))

    @on_side(1)
    def decode():
        state[0][...] = jnp.zeros_like(state[0])
        state[1][...] = jnp.full_like(state[1], MASKED)
        state[2][...] = jnp.zeros_like(state[2])
        pages = local_pages(z, chunks, shifts)
        add_pages(z, pages, plan_ref, decode_ref, state)


def second_kernel(z, groups, stored_plan_ref, prefill_ref, decode_ref, *refs):
    shifts = groups[1]
    refs, (plan_ref, plan_sem) = refs[:-2], refs[-2:]
    plan_copy = pltpu.make_async_copy(stored_plan_ref, plan_ref, plan_sem)
    plan_copy.start()
    before, new_ref, refs = refs[:3], refs[3], refs[4:]
    late, refs = refs[: len(shifts)], refs[len(shifts) :]
    state, (out_ref, held_ref, sems) = refs[:3], refs[3:]
    chunks = dict(zip(shifts, late))
    index = new_index(z, groups[0] + groups[1])
    column = lax.broadcasted_iota(jnp.int32, (1, LANES), 1)
    new_keys = jnp.concatenate(new_rows(z, new_ref, late, 0), axis=0)

    @on_side(0)
    def prefill():
        plan_copy.wait()
        visible = jnp.concatenate(prefix_visible(z, plan_ref, shifts), axis=0)
        keys = prefix_rows(z, chunks, shifts, 0)
        cached = len(keys) * z.page
        keys = jnp.concatenate(keys + new_rows(z, new_ref, late, 0), axis=0)
        values = prefix_rows(z, chunks, shifts, 1) + new_rows(z, new_ref, late, 1)
        values = jnp.concatenate(values, axis=0)
        copies = []
        for tile in range(z.prefill_tiles):
            query = lax.rem(column + tile * LANES, z.row_count)
            scores = score(keys, prefill_ref[tile])
            scores = jnp.concatenate(
                [
                    jnp.where(visible, scores[:cached], MASKED),
                    jnp.where(index <= query, scores[cached:], MASKED),
                ],
                axis=0,
            )
            part = merge(read(before, tile), soften(scores, values, z.scale), z.scale)
            held_ref[tile * LANES : (tile + 1) * LANES, :] = settle(part, held_ref.dtype)
            while len(copies) < min((tile + 1) * LANES // z.row_count, z.heads):
                h = len(copies)
                source = held_ref.at[pl.ds(h * z.row_count, z.row_count)]
                target = out_ref.at[:, pl.ds(h * z.head_dim, z.head_dim)]
                copies.append(pltpu.make_async_copy(source, target, sems.at[h]))
                copies[-1].start()
        for copy in copies:
            copy.wait()

    @on_side(1)
    def decode():
        owner = lax.rem(index, z.dec_rows)
        owner = jnp.where(index < z.row_count, owner, -1)
        step = index // z.dec_rows
        new_values = jnp.concatenate(new_rows(z, new_ref, late, 1), axis=0)
        for tile in range(z.decode_tiles):
            row, i = divmod(tile, z.row_tiles)
            query = (column + i * LANES) // z.heads
            visible = (owner == row) & (step <= query)
            scores = jnp.where(visible, score(new_keys, decode_ref[tile]), MASKED)
            part = soften(scores, new_values, z.scale)
            write(state, tile, merge(read(before, tile), part, z.scale))
        pages = local_pages(z, chunks, shifts)
        plan_copy.wait()
        add_pages(z, pages, plan_ref, decode_ref, state)


def last_kernel(z, groups, stored_plan_ref, decode_ref, early_ref, *refs):
    refs, (plan_ref, plan_sem) = refs[:-2], refs[-2:]
    plan_copy = pltpu.make_async_copy(stored_plan_ref, plan_ref, plan_sem)
    plan_copy.start()
    late, refs = refs[: len(groups[1])], refs[len(groups[1]) :]
    before, out_ref, refs = refs[:3], refs[4], refs[5:]
    state, (held_ref, rows_ref, sems) = refs[:3], refs[3:]

    @on_side(0)
    def prefill():
        plan_copy.wait()

    @on_side(1)
    def decode():
        for ref, value in zip(state, before):
            ref[...] = value[...]
        plan_copy.wait()
        places = [(early_ref, i * FIN_DEV * 2 * z.page) for i in range(len(groups[0]))]
        places += [(ref, z.prefix_pages * 2 * z.page) for ref in late]
        pages = landed_pages(z, places, groups[0] + groups[1])
        add_pages(z, pages, plan_ref, decode_ref, state)
        for tile in range(z.decode_tiles):
            held_ref[tile * LANES : (tile + 1) * LANES, :] = settle(read(state, tile), held_ref.dtype)
        copies = []
        for s in range(z.steps):
            span = pl.ds(s * z.dec_rows, z.dec_rows)
            for h in range(z.heads):
                rows = pl.ds(s * z.heads + h, z.dec_rows, stride=z.row_width)
                rows_ref[span, h * z.head_dim : (h + 1) * z.head_dim] = held_ref[rows, :].astype(
                    rows_ref.dtype
                )
            copies.append(
                pltpu.make_async_copy(rows_ref.at[span], out_ref.at[span], sems.at[s])
            )
            copies[-1].start()
        for copy in copies:
            copy.wait()


def call(kernel, z, shifts, name, keys, operands, outputs, scratch=(), aliases=None):
    spaces = {"smem": pltpu.SMEM, "vmem": pltpu.VMEM, "any": pl.ANY}
    spec = {key: pl.BlockSpec(memory_space=space) for key, space in spaces.items()}
    return pl.pallas_call(
        functools.partial(kernel, z, shifts),
        out_shape=[shape for _, shape in outputs],
        in_specs=[spec[key] for key, _ in operands],
        out_specs=[spec[key] for key, _ in outputs],
        scratch_shapes=list(scratch),
        input_output_aliases=aliases or {},
        compiler_params=pltpu.CompilerParams(vmem_limit_bytes=16 * 1024 * 1024),
        cost_estimate=pl.CostEstimate(
            flops=4 * z.tiles * LANES * keys * z.head_dim,
            bytes_accessed=2 * z.tiles * LANES * z.head_dim * 8,
            transcendentals=z.tiles * LANES * keys,
        ),
        name=name,
    )(*[value for _, value in operands])


def query_tiles(z, queries):
    by_head = queries.reshape((z.row_count, z.heads, z.head_dim)).transpose(1, 0, 2)
    by_head = by_head.reshape((-1, z.head_dim))
    spare = z.prefill_tiles * LANES - by_head.shape[0]
    by_head = jnp.pad(by_head, ((0, spare), (0, 0)))
    by_row = queries.reshape((z.steps, z.dec_rows, z.heads, z.head_dim)).transpose(1, 0, 2, 3)
    by_row = by_row.reshape((z.dec_rows, z.steps * z.heads, z.head_dim))
    by_row = jnp.pad(by_row, ((0, 0), (0, z.row_width - z.steps * z.heads), (0, 0)))
    return (
        by_head.reshape((z.prefill_tiles, LANES, z.head_dim)).transpose(0, 2, 1),
        by_row.reshape((z.decode_tiles, LANES, z.head_dim)).transpose(0, 2, 1),
    )


def hand_over(pages):
    return lax.ppermute(pages, "section", [(0, 1), (1, 0)])


def attend(z, inputs, queries, chunks, early, late):
    prefill, decode = query_tiles(z, queries)

    def shaped(space, shape, dtype):
        return (space, jax.ShapeDtypeStruct(shape, dtype))

    state = [
        shaped("vmem", (z.tiles, rows, LANES), jnp.float32) for rows in (z.head_dim, 1, 1)
    ]
    out = shaped("any", queries.shape, queries.dtype)
    plan, packed, new, *first = call(
        first_kernel,
        z,
        early,
        "early_pages",
        len(early) * z.page,
        [("smem", value) for value in inputs]
        + [("vmem", value) for value in (prefill, decode)]
        + [("vmem", chunks[d]) for d in early],
        [shaped("smem", (1 + 2 * z.slots,), jnp.int32)]
        + [
            shaped("vmem", (len(early) * rows, z.head_dim), queries.dtype)
            for rows in (FIN_DEV * 2 * z.page, 2 * z.new_pad)
        ]
        + state,
    )
    *waiting, plan = lax.optimization_barrier((*[chunks[d] for d in early + late], plan))
    landed = [hand_over(packed)] + [hand_over(chunk) for chunk in waiting[len(early) :]]
    *second, done = call(
        second_kernel,
        z,
        (early, late),
        "late_pages",
        len(late) * z.page + z.new_keys,
        [("any", plan)]
        + [("vmem", value) for value in (prefill, decode, *first, new)]
        + [("vmem", chunks[d]) for d in late],
        state + [out],
        [
            pltpu.VMEM((z.prefill_tiles * LANES, z.head_dim), queries.dtype),
            pltpu.SemaphoreType.DMA((z.heads,)),
            pltpu.SMEM(plan.shape, plan.dtype),
            pltpu.SemaphoreType.DMA,
        ],
    )
    operands = [("any", plan)]
    operands += [("vmem", value) for value in (decode, *landed, *second)]
    (result,) = call(
        last_kernel,
        z,
        (early, late),
        "landed_pages",
        z.page,
        operands + [("any", done)],
        [out],
        [pltpu.VMEM(shape.shape, shape.dtype) for _, shape in state]
        + [
            pltpu.VMEM((z.decode_tiles * LANES + z.row_width, z.head_dim), jnp.float32),
            pltpu.VMEM(queries.shape, queries.dtype),
            pltpu.SemaphoreType.DMA((z.steps,)),
            pltpu.SMEM(plan.shape, plan.dtype),
            pltpu.SemaphoreType.DMA,
        ],
        {len(operands): 0},
    )
    return result


def body(queries, fresh_key_value, key_value_page_store, prefix_len, page_table, context_len):
    tp = lax.axis_size("tp")
    store, fresh = key_value_page_store[0], fresh_key_value[0]
    z = Sizes(tp, store.shape, fresh.shape, queries.shape[1:], page_table.shape)

    def chunk_for(device):
        head = device * z.kv_heads // tp
        pages = lax.dynamic_index_in_dim(store, head, axis=2, keepdims=False)
        new = lax.dynamic_index_in_dim(fresh, head, axis=2, keepdims=False).transpose(1, 0, 2)
        new = jnp.pad(new, ((0, 0), (0, z.new_pad - z.new_rows), (0, 0)))
        return jnp.concatenate([pages.reshape((-1, z.head_dim)), new.reshape((-1, z.head_dim))])

    order = [2, tp - 2, 1] + list(range(3, tp - 2)) + [tp - 1]
    early, late = [0] + order[: tp // 2 - 1], order[tp // 2 - 1 :]
    chunks = {0: chunk_for(lax.axis_index("tp"))}
    for d in order:
        chunks[d] = lax.ppermute(chunk_for(z.target(d)), "tp", z.pairs(d))
    inputs = (prefix_len, page_table.T, context_len)
    return attend(z, inputs, queries[0], chunks, early, late)[None]


def solution(mesh):
    placed = (
        P(("pairs", "section"), None, "tp"),
        P(("pairs", "section"), "tp", None, None, None),
        P(("pairs", "section"), "tp", None, None, None, None),
        P("pairs"),
        P("pairs", None),
        P("pairs"),
    )
    return jax.shard_map(
        body,
        mesh=mesh,
        in_specs=placed,
        out_specs=P(("pairs", "section"), None, "tp"),
        check_vma=False,
    )
```
